32 devices in a mesh: dp: 2 (over core), seq: 4 (over z), tensor: 4 (over y, x).
Axes of the slice: x: 2, y: 2, z: 4, core: 2. Of those that a mesh axis runs over, the one named last changes fastest.
Arguments:
- query: bfloat16 [2, 1024, 2048], P('dp', 'seq', 'tensor'), may hold values from -1.75 to 1.75
- key_rows: bfloat16 [2, 1024, 2048], P('dp', 'seq', 'tensor'), may hold values from -1.75 to 1.75
- value: bfloat16 [2, 1024, 2048], P('dp', 'seq', 'tensor'), may hold values from -40 to 40
- gain: float32 [2048], P('tensor'), may hold values from 0.25 to 1.75
- grad_out: bfloat16 [2, 1024, 2048], P('dp', 'seq', 'tensor'), may hold values from -16 to 16
- start_offset: int32 [2, 16], P('dp', 'seq'), may hold values from 0 to 64, as said below
Outputs:
- attn_out: bfloat16 [2, 1024, 2048], P('dp', 'seq', 'tensor')
- grad_query: bfloat16 [2, 1024, 2048], P('dp', 'seq', 'tensor')
- grad_key: bfloat16 [2, 1024, 2048], P('dp', 'seq', 'tensor')
- grad_value: bfloat16 [2, 1024, 2048], P('dp', 'seq', 'tensor')
- grad_gain: float32 [2048], P('tensor')
The draws below stay inside these ranges and needn't reach their ends.
Inputs may be any that keep to these rules, and one draw needn't show every extreme that they name: `start_offset`: the position within its block of 64 positions at which a document starts; 64 when none starts in the block; every sequence begins a document at its first position.
All inputs are finite; a program needn't handle non-finite values.
Results may differ from the reference program's by a relative error of at most 0.0058.
Values sent between devices are 32-bit elements; how exact they have to be, the bound alone decides.
A program may use at most 64 MiB of HBM per device.

```python
import jax
import jax.numpy as jnp
from jax import lax

H = 16
DH = 128
TOK_DEV = 256
BLOCKS_DEV = 4
SEQS = 2
LENGTH = 1024
BLOCKS = 16
BLK = 64
CH = 2048
N_SEQ = 4


def draw_value(key, part):
    first, second = jax.random.split(key, 2)
    ladder = jnp.arange(H, dtype=jnp.float32) / (H - 1)
    jitter = jax.random.uniform(second, (H,), minval=0.0, maxval=1.0)
    scales = jnp.exp(jnp.log(3.0) * ladder + jnp.log(3.3) * jitter)
    base = jnp.clip(jax.random.normal(first, (SEQS, LENGTH, CH)), -4.0, 4.0)
    columns = jnp.repeat(scales, DH)
    return (base * columns[None, None, :]).astype(jnp.bfloat16)


def draw_grad_out(key, part):
    ramp = jnp.arange(LENGTH, dtype=jnp.float32) / (LENGTH - 1)
    rows = jnp.exp(jnp.log(3.0) * ramp)
    base = jnp.clip(jax.random.normal(key, (SEQS, LENGTH, CH)), -4.0, 4.0)
    return (base * rows[None, :, None]).astype(jnp.bfloat16)


def draw_start_offset(key, part):
    first, second, third = jax.random.split(key, 3)
    pick = jax.random.randint(first, (SEQS, BLOCKS), 0, 8)
    places = jax.random.randint(second, (SEQS, BLOCKS), 0, BLK)
    offsets = jnp.where(pick == 0, places, BLK)
    windows = BLOCKS // BLOCKS_DEV
    run_windows = 3 * windows // 4
    begin = jax.random.randint(third, (), 1, windows - run_windows + 1)
    window_of = jnp.arange(BLOCKS, dtype=jnp.int32) // BLOCKS_DEV
    inside = (window_of >= begin) & (window_of < begin + run_windows)
    last_row = jnp.arange(SEQS, dtype=jnp.int32) == SEQS - 1
    offsets = jnp.where(last_row[:, None] & inside[None, :], BLK, offsets)
    first_block = jnp.arange(BLOCKS, dtype=jnp.int32) == 0
    offsets = jnp.where(first_block[None, :], 0, offsets)
    return offsets.astype(jnp.int32)


def steps_of(stream_key, shape, cuts, smallest, top_value):
    level, own = 1.0, jax.random.fold_in(stream_key, 6)
    for axis_at, blocks in cuts:
        steps = jnp.exp(jax.random.uniform(jax.random.fold_in(own, axis_at), (blocks,), jnp.float32, smallest / len(cuts), top_value / len(cuts)))
        level = level * jnp.repeat(steps, shape[axis_at] // blocks).reshape([-1 if axis == axis_at else 1 for axis in range(len(shape))])
    return level


def noise(key, extent, spread, most, pieces=(), held_as=jnp.bfloat16):
    result = jax.random.normal(key, extent, jnp.float32) * spread
    if len(pieces) > 0:
        result = steps_of(key, extent, pieces, -0.22, 0.18) * result
    return jnp.clip(result, min=-most, max=most).astype(held_as)


def setup_inputs(seed: int = 0) -> dict:
    keys = jax.random.split(jax.random.key(seed), 7)
    query = noise(keys[0], (SEQS, LENGTH, CH), 0.3, 1.75, ((0, 2), (1, 4), (2, 4)))
    key_rows = noise(keys[1], (SEQS, LENGTH, CH), 0.3, 1.75, ((0, 2), (1, 4), (2, 4)))
    value = draw_value(jax.random.fold_in(keys[6], 71), 0)
    gain = jnp.clip(1.0 + 0.15 * jax.random.normal(keys[3], (CH,), jnp.float32), 0.25, 1.75)
    grad_out = draw_grad_out(jax.random.fold_in(keys[6], 71), 0)
    start_offset = draw_start_offset(jax.random.fold_in(keys[6], 71), 0)
    return dict(query=query, key_rows=key_rows, value=value, gain=gain, grad_out=grad_out, start_offset=start_offset)


eps_value = 1e-05

def segment_rows(offsets, length_dev):
    positions = jnp.arange(length_dev, dtype=jnp.int32)
    block_starts = jnp.arange(offsets.shape[0], dtype=jnp.int32) * BLK + offsets
    present = offsets < BLK
    covered = (block_starts[None, :] <= positions[:, None]) & present[None, :]
    labels = lax.optimization_barrier(jnp.sum(covered.astype(jnp.int32), axis=1))
    allowed = (labels[:, None] == labels[None, :]) & (positions[None, :] <= positions[:, None])
    starts = jnp.sum(present.astype(jnp.int32))
    return (labels, starts, allowed)

def rounded(values):
    return lax.optimization_barrier(values.astype(jnp.bfloat16)).astype(jnp.float32)

def widened(values):
    return values.astype(jnp.float32)

def prefix_step(carry, item):
    part, flag = item
    return (jnp.where(flag > 0, part, carry + part), carry)

def run_prefix(parts, flags, backward):
    start_state = jnp.zeros((H, DH, DH), jnp.float32)
    final_state, outputs = lax.scan(prefix_step, start_state, (parts, flags), reverse=backward)
    return outputs

def reference(query, key_rows, value, gain, grad_out, start_offset):
    blocks_all = SEQS * N_SEQ
    query_blocks = query.reshape(blocks_all, TOK_DEV, H, DH)
    key_blocks = key_rows.reshape(blocks_all, TOK_DEV, H, DH)
    value_blocks = value.reshape(blocks_all, TOK_DEV, H, DH)
    grad_blocks = grad_out.reshape(blocks_all, TOK_DEV, CH)
    offset_blocks = start_offset.reshape(blocks_all, BLOCKS_DEV)

    def forward_block(items):
        query_one, key_one, value_one, offsets = items
        labels, starts, allowed = segment_rows(offsets, TOK_DEV)
        scores = jnp.einsum('thd,shd->hts', widened(query_one), widened(key_one))
        weights = rounded(jnp.where(allowed[None], scores, 0.0))
        local_out = jnp.einsum('hts,shd->thd', weights, widened(value_one))
        tail_keys = jnp.where((labels == starts)[:, None, None], widened(key_one), 0.0)
        tail_state = jnp.einsum('shi,shj->hij', tail_keys, widened(value_one))
        return (local_out, tail_state, (starts > 0).astype(jnp.int32))
    local_out, tail_state, reset = lax.map(forward_block, (query_blocks, key_blocks, value_blocks, offset_blocks))
    tails = tail_state.reshape(SEQS, N_SEQ, H, DH, DH)
    resets = reset.reshape(SEQS, N_SEQ)
    incoming = jnp.stack([run_prefix(tails[index], resets[index], False) for index in range(SEQS)])
    incoming = incoming.reshape(blocks_all, H, DH, DH)

    def middle_block(items):
        query_one, local_one, incoming_one, grad_one, offsets = items
        labels, starts, allowed = segment_rows(offsets, TOK_DEV)
        carried = rounded(incoming_one)
        head_query = jnp.where((labels == 0)[:, None, None], widened(query_one), 0.0)
        carried_out = jnp.einsum('thi,hij->thj', head_query, carried)
        attended = (local_one + carried_out).reshape(TOK_DEV, CH)
        inverse = lax.rsqrt(lax.optimization_barrier(jnp.sum(attended * attended, axis=1)) / CH + eps_value)
        normed = attended * inverse[:, None]
        upstream = widened(grad_one)
        scaled = gain[None, :] * upstream
        output = (gain[None, :] * normed).astype(jnp.bfloat16)
        product_total = lax.optimization_barrier(jnp.sum(scaled * normed, axis=1))
        grad_wide = rounded(inverse[:, None] * (scaled - normed * (product_total / CH)[:, None]))
        gain_part = lax.optimization_barrier(jnp.sum(upstream * normed, axis=0))
        grad_state = jnp.einsum('thi,thj->hij', head_query, grad_wide.reshape(TOK_DEV, H, DH))
        return (output, grad_wide, gain_part, grad_state)
    output, grad_wide, gain_parts, grad_state = lax.map(middle_block, (query_blocks, local_out, incoming, grad_blocks, offset_blocks))
    states = grad_state.reshape(SEQS, N_SEQ, H, DH, DH)
    later = jnp.stack([run_prefix(states[index], resets[index], True) for index in range(SEQS)])
    later = later.reshape(blocks_all, H, DH, DH)

    def backward_block(items):
        query_one, key_one, value_one, grad_one, incoming_one, later_one, offsets = items
        labels, starts, allowed = segment_rows(offsets, TOK_DEV)
        query_wide = widened(query_one)
        key_wide = widened(key_one)
        value_wide = widened(value_one)
        grad_heads = grad_one.reshape(TOK_DEV, H, DH)
        scores = jnp.einsum('thd,shd->hts', query_wide, key_wide)
        weights = rounded(jnp.where(allowed[None], scores, 0.0))
        grad_scores = jnp.einsum('thd,shd->hts', grad_heads, value_wide)
        grad_weights = rounded(jnp.where(allowed[None], grad_scores, 0.0))
        head_mask = (labels == 0)[:, None, None]
        tail_mask = (labels == starts)[:, None, None]
        carried = rounded(incoming_one)
        later_half = rounded(later_one)
        head_grad = jnp.where(head_mask, grad_heads, 0.0)
        tail_keys = jnp.where(tail_mask, key_wide, 0.0)
        tail_values = jnp.where(tail_mask, value_wide, 0.0)
        grad_query = jnp.einsum('hts,shd->thd', grad_weights, key_wide) + jnp.einsum('thj,hij->thi', head_grad, carried)
        grad_key = jnp.einsum('hts,thd->shd', grad_weights, query_wide) + jnp.einsum('shj,hij->shi', tail_values, later_half)
        grad_value = jnp.einsum('hts,thd->shd', weights, grad_heads) + jnp.einsum('shi,hij->shj', tail_keys, later_half)
        return (grad_query.reshape(TOK_DEV, CH).astype(jnp.bfloat16), grad_key.reshape(TOK_DEV, CH).astype(jnp.bfloat16), grad_value.reshape(TOK_DEV, CH).astype(jnp.bfloat16))
    grad_query, grad_key, grad_value = lax.map(backward_block, (query_blocks, key_blocks, value_blocks, grad_wide, incoming, later, offset_blocks))
    shape_all = (SEQS, LENGTH, CH)
    grad_gain = lax.optimization_barrier(jnp.sum(gain_parts, axis=0))
    return (output.reshape(shape_all), grad_query.reshape(shape_all), grad_key.reshape(shape_all), grad_value.reshape(shape_all), grad_gain)
```

```python
import functools

import jax
import jax.numpy as jnp
from jax import lax
from jax.experimental import pallas as pl
from jax.experimental.pallas import tpu as pltpu
from jax.sharding import PartitionSpec as P

DH = 128
BLK = 64
CH = 2048
EPS = 1e-05
CUTS = 2

MESH = pl.DeviceIdType.MESH
F32 = jnp.float32
BF16 = jnp.bfloat16


def dot(a, b, over_a, over_b):
    return lax.dot_general(a, b, (((over_a,), (over_b,)), ((), ())), preferred_element_type=F32)


def kernel(
    sizes, off_ref, gain_ref, q_hbm, k_hbm, v_hbm, g_hbm,
    out_hbm, gq_hbm, gk_hbm, gv_hbm, gg_ref,
    q_ref, k_ref, v_ref, g_ref, out_ref, gq_ref, gk_ref, gv_ref,
    allow_ref, wts_ref, att_ref, pre_ref, pk_ref, pv_ref,
    fsend, frecv, bsend, brecv, stats, gains,
    in_sem, out_sem, fs_sem, fr_sem, bs_sem, br_sem, ss_sem, sr_sem, gs_sem, gr_sem,
):
    n_dp, n_seq, n_ten = sizes
    group = n_dp * n_seq
    length, width = q_ref.shape
    heads = width // DH
    rows = DH // CUTS
    place = lax.axis_index("seq")
    ten = lax.axis_index("tensor")
    mine = lax.axis_index("dp") * n_seq + place
    first, last = place == 0, place == n_seq - 1

    loads = [
        pltpu.make_async_copy(src, dst, in_sem.at[i])
        for i, (src, dst) in enumerate(((k_hbm, k_ref), (v_hbm, v_ref), (q_hbm, q_ref), (g_hbm, g_ref)))
    ]
    for load in loads:
        load.start()

    barrier = pltpu.get_barrier_semaphore()

    def peer(turn):
        other = lax.rem(mine + turn, group)
        return other, {"dp": lax.div(other, n_seq), "seq": lax.rem(other, n_seq)}

    def greet(turn, carry):
        pl.semaphore_signal(barrier, inc=1, device_id=peer(turn)[1], device_id_type=MESH)
        return carry

    lax.fori_loop(1, group, greet, 0)
    for turn in range(1, n_ten):
        pl.semaphore_signal(
            barrier, inc=1, device_id={"tensor": lax.rem(ten + turn, n_ten)}, device_id_type=MESH
        )

    def cols(h):
        return pl.ds(h * DH, DH)

    def forward(c):
        h, at = c // CUTS, pl.ds((c % CUTS) * rows, rows)
        return pltpu.make_async_remote_copy(
            src_ref=fsend.at[h, at], dst_ref=frecv.at[h, at],
            send_sem=fs_sem.at[c], recv_sem=fr_sem.at[c],
            device_id={"seq": place + 1}, device_id_type=MESH,
        )

    def backward(c):
        h, at = c // CUTS, pl.ds((c % CUTS) * rows, rows)
        return pltpu.make_async_remote_copy(
            src_ref=bsend.at[h, at], dst_ref=brecv.at[h, at],
            send_sem=bs_sem.at[c], recv_sem=br_sem.at[c],
            device_id={"seq": place - 1}, device_id_type=MESH,
        )

    starts_at = []
    starts = jnp.int32(0)
    for j in range(off_ref.shape[1]):
        offset = off_ref[0, j]
        starts_at.append(jnp.where(offset < BLK, j * BLK + offset, length))
        starts = starts + jnp.where(offset < BLK, 1, 0)

    def labels(positions):
        total = jnp.zeros(positions.shape, jnp.int32)
        for at in starts_at:
            total = total + jnp.where(positions >= at, 1, 0)
        return total

    label = labels(lax.broadcasted_iota(jnp.int32, (length, DH), 0))
    head_mask = jnp.where(label == 0, 1.0, 0.0).astype(BF16)
    tail_mask = jnp.where(label == starts, 1.0, 0.0).astype(BF16)
    keep = jnp.full((rows, DH), starts, jnp.int32) == 0

    loads[0].wait()
    loads[1].wait()
    for h in range(heads):
        fsend[h] = dot(k_ref[:, cols(h)] * tail_mask, v_ref[:, cols(h)], 0, 0)
        if h == 0:
            pl.semaphore_wait(barrier, group - 1 + n_ten - 1)

        @pl.when(first & (n_seq > 1))
        def _():
            for part in range(CUTS):
                forward(h * CUTS + part).start()

    rows_at = lax.broadcasted_iota(jnp.int32, (length, length), 0)
    cols_at = lax.broadcasted_iota(jnp.int32, (length, length), 1)
    allow_ref[...] = jnp.where(
        (labels(rows_at) == labels(cols_at)) & (cols_at <= rows_at), 1.0, 0.0
    )

    @pl.when(first)
    def _():
        frecv[...] = jnp.zeros_like(frecv)

    @pl.when(last)
    def _():
        brecv[...] = jnp.zeros_like(brecv)

    loads[2].wait()
    loads[3].wait()

    square = jnp.zeros((length, DH), F32)
    raw = jnp.zeros((length, DH), F32)
    for h in range(heads):
        query = q_ref[:, cols(h)]
        scores = dot(query, k_ref[:, cols(h)], 1, 1)
        weights = (scores * allow_ref[...]).astype(BF16)
        wts_ref[h] = weights
        local_out = dot(weights, v_ref[:, cols(h)], 1, 0)

        for part in range(CUTS):
            c = h * CUTS + part

            @pl.when(jnp.logical_not(first))
            def _():
                forward(c).wait_recv()

                @pl.when(jnp.logical_not(last))
                def _():
                    at = pl.ds(part * rows, rows)
                    fsend[h, at] = fsend[h, at] + jnp.where(keep, frecv[h, at], 0.0)
                    forward(c).start()

        carried = frecv[h].astype(BF16)
        attended = local_out + dot(query * head_mask, carried, 1, 0)
        att_ref[:, cols(h)] = attended
        square = square + attended * attended
        raw = raw + gain_ref[:, cols(h)] * g_ref[:, cols(h)].astype(F32) * attended

    stats[ten, 0:1, :] = jnp.sum(square.T, axis=0, keepdims=True)
    stats[ten, 1:2, :] = jnp.sum(raw.T, axis=0, keepdims=True)

    def exchange(turn, slot):
        return pltpu.make_async_remote_copy(
            src_ref=stats.at[slot], dst_ref=stats.at[slot],
            send_sem=ss_sem.at[turn], recv_sem=sr_sem.at[slot],
            device_id={"tensor": lax.rem(ten + turn, n_ten)}, device_id_type=MESH,
        )

    for turn in range(1, n_ten):
        exchange(turn, ten).start()
    for turn in range(1, n_ten):
        exchange(turn, lax.rem(ten + turn, n_ten)).wait_recv()
    totals = stats[0]
    for t in range(1, n_ten):
        totals = totals + stats[t]
    inverse = lax.rsqrt(totals[0:1, :] / CH + EPS)
    slope = inverse * inverse * (totals[1:2, :] / CH)
    inverse = jnp.broadcast_to(inverse, (DH, length)).T
    slope = jnp.broadcast_to(slope, (DH, length)).T

    for h in range(heads):
        upstream = g_ref[:, cols(h)].astype(F32)
        pre = inverse * (gain_ref[:, cols(h)] * upstream - att_ref[:, cols(h)] * slope)
        pre = pre.astype(BF16)
        pre_ref[:, cols(h)] = pre
        bsend[h] = dot(q_ref[:, cols(h)] * head_mask, pre, 0, 0)

        @pl.when(last & (n_seq > 1))
        def _():
            for part in range(CUTS):
                backward(h * CUTS + part).start()

    def store(index, h, src, dst):
        return pltpu.make_async_copy(src.at[:, cols(h)], dst.at[:, cols(h)], out_sem.at[index, h])

    for h in range(heads):
        normed = att_ref[:, cols(h)] * inverse
        out_ref[:, cols(h)] = (gain_ref[:, cols(h)] * normed).astype(BF16)
        store(0, h, out_ref, out_hbm).start()
        gains[mine, :, cols(h)] = jnp.sum(
            g_ref[:, cols(h)].astype(F32) * normed, axis=0, keepdims=True
        )

    def send_gain(turn, slot):
        return pltpu.make_async_remote_copy(
            src_ref=gains.at[slot], dst_ref=gains.at[slot],
            send_sem=gs_sem.at[turn], recv_sem=gr_sem.at[slot],
            device_id=peer(turn)[1], device_id_type=MESH,
        )

    def start_gain(turn, carry):
        send_gain(turn, mine).start()
        return carry

    lax.fori_loop(1, group, start_gain, 0)

    for h in range(heads):
        query, key, value = q_ref[:, cols(h)], k_ref[:, cols(h)], v_ref[:, cols(h)]
        pre = pre_ref[:, cols(h)]
        grad_weights = (dot(pre, value, 1, 1) * allow_ref[...]).astype(BF16)
        gq = dot(grad_weights, key, 1, 0) + dot(pre * head_mask, frecv[h].astype(BF16), 1, 1)
        gq_ref[:, cols(h)] = gq.astype(BF16)
        store(1, h, gq_ref, gq_hbm).start()
        pk_ref[...] = dot(grad_weights, query, 0, 0)
        pv_ref[...] = dot(wts_ref[h], pre, 0, 0)

        for part in range(CUTS):
            c = h * CUTS + part

            @pl.when(jnp.logical_not(last))
            def _():
                backward(c).wait_recv()

                @pl.when(jnp.logical_not(first))
                def _():
                    at = pl.ds(part * rows, rows)
                    bsend[h, at] = bsend[h, at] + jnp.where(keep, brecv[h, at], 0.0)
                    backward(c).start()

        later = brecv[h].astype(BF16)
        gk_ref[:, cols(h)] = (pk_ref[...] + dot(value * tail_mask, later, 1, 1)).astype(BF16)
        store(2, h, gk_ref, gk_hbm).start()
        gv_ref[:, cols(h)] = (pv_ref[...] + dot(key * tail_mask, later, 1, 0)).astype(BF16)
        store(3, h, gv_ref, gv_hbm).start()

    def wait_gain(turn, carry):
        send_gain(turn, peer(turn)[0]).wait_recv()
        return carry

    lax.fori_loop(1, group, wait_gain, 0)
    gg_ref[...] = lax.fori_loop(
        0, group, lambda i, total: total + gains[i], jnp.zeros(gg_ref.shape, F32)
    )

    def sent_gain(turn, carry):
        send_gain(turn, mine).wait_send()
        return carry

    lax.fori_loop(1, group, sent_gain, 0)
    for turn in range(1, n_ten):
        exchange(turn, ten).wait_send()

    @pl.when(jnp.logical_not(last))
    def _():
        for c in range(heads * CUTS):
            forward(c).wait_send()

    @pl.when(jnp.logical_not(first))
    def _():
        for c in range(heads * CUTS):
            backward(c).wait_send()

    for index, (src, dst) in enumerate(
        ((out_ref, out_hbm), (gq_ref, gq_hbm), (gk_ref, gk_hbm), (gv_ref, gv_hbm))
    ):
        for h in range(heads):
            store(index, h, src, dst).wait()


def solution(mesh):
    sizes = (mesh.shape["dp"], mesh.shape["seq"], mesh.shape["tensor"])

    def shards(query, key_rows, value, gain, grad_out, start_offset):
        _, length, width = query.shape
        heads = width // DH
        group = sizes[0] * sizes[1]
        cuts = heads * CUTS
        whole = pl.BlockSpec(memory_space=pl.ANY)
        vmem = pl.BlockSpec(memory_space=pltpu.VMEM)
        rows = jax.ShapeDtypeStruct((length, width), BF16)
        dma = pltpu.SemaphoreType.DMA
        flat = lambda a: a.reshape(length, width)
        *outs, grad_gain = pl.pallas_call(
            functools.partial(kernel, sizes),
            out_shape=(rows,) * 4 + (jax.ShapeDtypeStruct((1, width), F32),),
            in_specs=[pl.BlockSpec(memory_space=pltpu.SMEM), vmem] + [whole] * 4,
            out_specs=(whole,) * 4 + (vmem,),
            scratch_shapes=[pltpu.VMEM((length, width), BF16)] * 8
            + [
                pltpu.VMEM((length, length), F32),
                pltpu.VMEM((heads, length, length), BF16),
                pltpu.VMEM((length, width), F32),
                pltpu.VMEM((length, width), BF16),
                pltpu.VMEM((length, DH), F32),
                pltpu.VMEM((length, DH), F32),
            ]
            + [pltpu.VMEM((heads, DH, DH), F32)] * 4
            + [pltpu.VMEM((sizes[2], 2, length), F32), pltpu.VMEM((group, 1, width), F32)]
            + [dma((4,)), dma((4, heads)), dma((cuts,)), dma((cuts,)), dma((cuts,)), dma((cuts,))]
            + [dma((sizes[2],)), dma((sizes[2],)), dma((group,)), dma((group,))],
            compiler_params=pltpu.CompilerParams(
                collective_id=0, has_side_effects=True, vmem_limit_bytes=40 * 1024 * 1024
            ),
        )(start_offset, gain.reshape(1, width), flat(query), flat(key_rows), flat(value), flat(grad_out))
        return tuple(a.reshape(1, length, width) for a in outs) + (grad_gain.reshape(width),)

    split = P("dp", "seq", "tensor")
    return jax.shard_map(
        shards,
        mesh=mesh,
        in_specs=(split, split, split, P("tensor"), split, P("dp", "seq")),
        out_specs=(split, split, split, split, P("tensor")),
        check_vma=False,
    )
```

```python
import functools

import jax
import jax.numpy as jnp
from jax import lax
from jax.experimental import pallas as pl
from jax.experimental.pallas import tpu as pltpu
from jax.sharding import PartitionSpec as P

DH = 128
BLK = 64
CH = 2048
EPS = 1e-05
CUTS = 2

MESH = pl.DeviceIdType.MESH
F32 = jnp.float32
BF16 = jnp.bfloat16


def dot(a, b, over_a, over_b):
    return lax.dot_general(a, b, (((over_a,), (over_b,)), ((), ())), preferred_element_type=F32)


def kernel(
    sizes, off_hbm, gain_hbm, q_hbm, k_hbm, v_hbm, g_hbm,
    out_ref, gq_ref, gk_ref, gv_ref, gg_ref,
    off_ref, gain_ref, q_ref, k_ref, v_ref, g_ref,
    allow_ref, head_ref, tail_ref, wts_ref, att_ref, pre_ref, pk_ref, pv_ref, sq_ref, raw_ref,
    fsend, frecv, bsend, brecv, stats, gains,
    in_sem, fs_sem, fr_sem, bs_sem, br_sem, ss_sem, sr_sem, gs_sem, gr_sem,
):
    n_dp, n_seq, n_ten = sizes
    group = n_dp * n_seq
    length, width = q_ref.shape
    heads = width // DH
    rows = DH // CUTS
    place = lax.axis_index("seq")
    ten = lax.axis_index("tensor")
    mine = lax.axis_index("dp") * n_seq + place
    first, last = place == 0, place == n_seq - 1

    loads = [
        pltpu.make_async_copy(src, dst, in_sem.at[i])
        for i, (src, dst) in enumerate(
            (
                (off_hbm, off_ref), (k_hbm, k_ref), (v_hbm, v_ref),
                (q_hbm, q_ref), (g_hbm, g_ref), (gain_hbm, gain_ref),
            )
        )
    ]
    for load in loads:
        load.start()

    barrier = pltpu.get_barrier_semaphore()

    def peer(turn):
        other = lax.rem(mine + turn, group)
        return other, {"dp": lax.div(other, n_seq), "seq": lax.rem(other, n_seq)}

    def greet(turn, carry):
        pl.semaphore_signal(barrier, inc=1, device_id=peer(turn)[1], device_id_type=MESH)
        return carry

    lax.fori_loop(1, group, greet, 0)
    for turn in range(1, n_ten):
        pl.semaphore_signal(
            barrier, inc=1, device_id={"tensor": lax.rem(ten + turn, n_ten)}, device_id_type=MESH
        )

    def cols(h):
        return pl.ds(h * DH if isinstance(h, int) else pl.multiple_of(h * DH, DH), DH)

    def piece(part):
        return pl.ds(part * rows, rows)

    def forward(h, part):
        return pltpu.make_async_remote_copy(
            src_ref=fsend.at[h, piece(part)], dst_ref=frecv.at[h, piece(part)],
            send_sem=fs_sem.at[h, part], recv_sem=fr_sem.at[h, part],
            device_id={"seq": place + 1}, device_id_type=MESH,
        )

    def backward(h, part):
        return pltpu.make_async_remote_copy(
            src_ref=bsend.at[h, piece(part)], dst_ref=brecv.at[h, piece(part)],
            send_sem=bs_sem.at[h, part], recv_sem=br_sem.at[h, part],
            device_id={"seq": place - 1}, device_id_type=MESH,
        )

    def each_head(body):
        def step(h, carry):
            body(h)
            return carry

        lax.fori_loop(0, heads, step, 0)

    loads[0].wait()
    starts_at = []
    starts = jnp.int32(0)
    for j in range(off_ref.shape[1]):
        offset = off_ref[0, j]
        starts_at.append(jnp.where(offset < BLK, j * BLK + offset, length))
        starts = starts + jnp.where(offset < BLK, 1, 0)

    def labels(positions):
        total = jnp.zeros(positions.shape, jnp.int32)
        for at in starts_at:
            total = total + jnp.where(positions >= at, 1, 0)
        return total

    label = labels(lax.broadcasted_iota(jnp.int32, (length, DH), 0))
    head_ref[...] = jnp.where(label == 0, 1.0, 0.0).astype(BF16)
    tail_ref[...] = jnp.where(label == starts, 1.0, 0.0).astype(BF16)

    def passed(own, come):
        keep = jnp.full(come.shape, starts, jnp.int32) == 0
        return own + jnp.where(keep, come, 0.0)

    loads[1].wait()
    loads[2].wait()

    def tail(h):
        fsend[h] = dot(k_ref[:, cols(h)] * tail_ref[...], v_ref[:, cols(h)], 0, 0)

    def launch(h):
        @pl.when(first & (n_seq > 1))
        def _():
            for part in range(CUTS):
                forward(h, part).start()

    tail(0)
    pl.semaphore_wait(barrier, group - 1 + n_ten - 1)
    launch(0)

    def tails(h, carry):
        tail(h)
        launch(h)
        return carry

    lax.fori_loop(1, heads, tails, 0)

    rows_at = lax.broadcasted_iota(jnp.int32, (length, length), 0)
    cols_at = lax.broadcasted_iota(jnp.int32, (length, length), 1)
    allow_ref[...] = jnp.where(
        (labels(rows_at) == labels(cols_at)) & (cols_at <= rows_at), 1.0, 0.0
    )

    @pl.when(first)
    def _():
        frecv[...] = jnp.zeros_like(frecv)

    @pl.when(last)
    def _():
        brecv[...] = jnp.zeros_like(brecv)

    sq_ref[...] = jnp.zeros_like(sq_ref)
    raw_ref[...] = jnp.zeros_like(raw_ref)
    for load in loads[3:]:
        load.wait()

    def relay_right(h, part):
        @pl.when(jnp.logical_not(first))
        def _():
            forward(h, part).wait_recv()

            @pl.when(jnp.logical_not(last))
            def _():
                fsend[h, piece(part)] = passed(fsend[h, piece(part)], frecv[h, piece(part)])
                forward(h, part).start()

    def attend(h):
        relay_right(h, 0)
        scores = dot(q_ref[:, cols(h)], k_ref[:, cols(h)], 1, 1)
        wts_ref[h] = (scores * allow_ref[...]).astype(BF16)
        att_ref[:, cols(h)] = dot(wts_ref[h], v_ref[:, cols(h)], 1, 0)
        for part in range(1, CUTS):
            relay_right(h, part)
        attended = att_ref[:, cols(h)] + dot(
            q_ref[:, cols(h)] * head_ref[...], frecv[h].astype(BF16), 1, 0
        )
        att_ref[:, cols(h)] = attended
        sq_ref[...] = sq_ref[...] + attended * attended
        raw_ref[...] = raw_ref[...] + gain_ref[:, cols(h)] * g_ref[:, cols(h)].astype(F32) * attended

    each_head(attend)

    stats[ten, 0:1, :] = jnp.sum(sq_ref[...].T, axis=0, keepdims=True)
    stats[ten, 1:2, :] = jnp.sum(raw_ref[...].T, axis=0, keepdims=True)

    def exchange(turn, slot):
        return pltpu.make_async_remote_copy(
            src_ref=stats.at[slot], dst_ref=stats.at[slot],
            send_sem=ss_sem.at[turn], recv_sem=sr_sem.at[slot],
            device_id={"tensor": lax.rem(ten + turn, n_ten)}, device_id_type=MESH,
        )

    for turn in range(1, n_ten):
        exchange(turn, ten).start()
    for turn in range(1, n_ten):
        exchange(turn, lax.rem(ten + turn, n_ten)).wait_recv()
    totals = stats[0]
    for t in range(1, n_ten):
        totals = totals + stats[t]
    inverse = lax.rsqrt(totals[0:1, :] / CH + EPS)
    slope = inverse * inverse * (totals[1:2, :] / CH)
    sq_ref[...] = jnp.broadcast_to(inverse, (DH, length)).T
    raw_ref[...] = jnp.broadcast_to(slope, (DH, length)).T

    def before_norm(h):
        upstream = g_ref[:, cols(h)].astype(F32)
        pre = sq_ref[...] * (gain_ref[:, cols(h)] * upstream - att_ref[:, cols(h)] * raw_ref[...])
        pre = pre.astype(BF16)
        pre_ref[:, cols(h)] = pre
        bsend[h] = dot(q_ref[:, cols(h)] * head_ref[...], pre, 0, 0)

        @pl.when(last & (n_seq > 1))
        def _():
            for part in range(CUTS):
                backward(h, part).start()

    each_head(before_norm)

    def after_norm(h):
        normed = att_ref[:, cols(h)] * sq_ref[...]
        out_ref[:, cols(h)] = (gain_ref[:, cols(h)] * normed).astype(BF16)
        gains[mine, :, cols(h)] = jnp.sum(
            g_ref[:, cols(h)].astype(F32) * normed, axis=0, keepdims=True
        )

    for h in range(heads):
        after_norm(h)

    def send_gain(turn, slot):
        return pltpu.make_async_remote_copy(
            src_ref=gains.at[slot], dst_ref=gains.at[slot],
            send_sem=gs_sem.at[turn], recv_sem=gr_sem.at[slot],
            device_id=peer(turn)[1], device_id_type=MESH,
        )

    def start_gain(turn, carry):
        send_gain(turn, mine).start()
        return carry

    lax.fori_loop(1, group, start_gain, 0)

    def relay_left(h, part):
        @pl.when(jnp.logical_not(last))
        def _():
            backward(h, part).wait_recv()

            @pl.when(jnp.logical_not(first))
            def _():
                bsend[h, piece(part)] = passed(bsend[h, piece(part)], brecv[h, piece(part)])
                backward(h, part).start()

    def local_query(h):
        pre = pre_ref[:, cols(h)]
        grad_weights = (dot(pre, v_ref[:, cols(h)], 1, 1) * allow_ref[...]).astype(BF16)
        gq = dot(grad_weights, k_ref[:, cols(h)], 1, 0)
        gq = gq + dot(pre * head_ref[...], frecv[h].astype(BF16), 1, 1)
        gq_ref[:, cols(h)] = gq.astype(BF16)
        pk_ref[:, cols(h)] = dot(grad_weights, q_ref[:, cols(h)], 0, 0)

    def local_value(h):
        pv_ref[:, cols(h)] = dot(wts_ref[h], pre_ref[:, cols(h)], 0, 0)

    def finish(h):
        later = brecv[h].astype(BF16)
        gk = pk_ref[:, cols(h)] + dot(v_ref[:, cols(h)] * tail_ref[...], later, 1, 1)
        gk_ref[:, cols(h)] = gk.astype(BF16)
        gv = pv_ref[:, cols(h)] + dot(k_ref[:, cols(h)] * tail_ref[...], later, 1, 0)
        gv_ref[:, cols(h)] = gv.astype(BF16)

    @pl.when(first | last)
    def _():
        def local(h):
            local_query(h)
            local_value(h)

        each_head(local)

        def arrive(h):
            for part in range(CUTS):
                relay_left(h, part)
            finish(h)

        each_head(arrive)

    @pl.when(jnp.logical_not(first | last))
    def _():
        def both(h):
            relay_left(h, 0)
            local_query(h)
            for part in range(1, CUTS):
                relay_left(h, part)
            local_value(h)
            finish(h)

        each_head(both)

    def wait_gain(turn, carry):
        send_gain(turn, peer(turn)[0]).wait_recv()
        return carry

    lax.fori_loop(1, group, wait_gain, 0)
    gg_ref[...] = lax.fori_loop(
        0, group, lambda i, total: total + gains[i], jnp.zeros(gg_ref.shape, F32)
    )

    def sent_gain(turn, carry):
        send_gain(turn, mine).wait_send()
        return carry

    lax.fori_loop(1, group, sent_gain, 0)
    for turn in range(1, n_ten):
        exchange(turn, ten).wait_send()

    @pl.when(jnp.logical_not(last))
    def _():
        for h in range(heads):
            for part in range(CUTS):
                forward(h, part).wait_send()

    @pl.when(jnp.logical_not(first))
    def _():
        for h in range(heads):
            for part in range(CUTS):
                backward(h, part).wait_send()


def hand_out(*refs):
    count = len(refs) // 2
    copies = [
        pltpu.make_async_copy(refs[i], refs[count + i], refs[-1].at[i]) for i in range(count)
    ]
    for copy in copies:
        copy.start()
    for copy in copies:
        copy.wait()


def solution(mesh):
    sizes = (mesh.shape["dp"], mesh.shape["seq"], mesh.shape["tensor"])

    def shards(query, key_rows, value, gain, grad_out, start_offset):
        _, length, width = query.shape
        heads = width // DH
        group = sizes[0] * sizes[1]
        hbm = pl.BlockSpec(memory_space=pltpu.HBM)
        vmem = pl.BlockSpec(memory_space=pltpu.VMEM)
        rows = jax.ShapeDtypeStruct((length, width), BF16)
        shapes = (rows,) * 4 + (jax.ShapeDtypeStruct((1, width), F32),)
        dma = pltpu.SemaphoreType.DMA
        flat = lambda a: a.reshape(length, width)
        outs = pl.pallas_call(
            functools.partial(kernel, sizes),
            out_shape=tuple(pltpu.VMEM(a.shape, a.dtype) for a in shapes),
            in_specs=[hbm] * 6,
            out_specs=(vmem,) * 5,
            scratch_shapes=[pltpu.SMEM(start_offset.shape, jnp.int32), pltpu.VMEM((1, width), F32)]
            + [pltpu.VMEM((length, width), BF16)] * 4
            + [
                pltpu.VMEM((length, length), F32),
                pltpu.VMEM((length, DH), BF16),
                pltpu.VMEM((length, DH), BF16),
                pltpu.VMEM((heads, length, length), BF16),
                pltpu.VMEM((length, width), F32),
                pltpu.VMEM((length, width), BF16),
                pltpu.VMEM((length, width), F32),
                pltpu.VMEM((length, width), F32),
                pltpu.VMEM((length, DH), F32),
                pltpu.VMEM((length, DH), F32),
            ]
            + [pltpu.VMEM((heads, DH, DH), F32)] * 4
            + [pltpu.VMEM((sizes[2], 2, length), F32), pltpu.VMEM((group, 1, width), F32)]
            + [dma((6,))] + [dma((heads, CUTS))] * 4
            + [dma((sizes[2],)), dma((sizes[2],)), dma((group,)), dma((group,))],
            compiler_params=pltpu.CompilerParams(
                collective_id=0, has_side_effects=True, vmem_limit_bytes=61 * 1024 * 1024
            ),
        )(start_offset, gain.reshape(1, width), flat(query), flat(key_rows), flat(value), flat(grad_out))
        *outs, grad_gain = pl.pallas_call(
            hand_out,
            out_shape=shapes,
            in_specs=[pl.BlockSpec(memory_space=pl.ANY)] * 5,
            out_specs=(hbm,) * 5,
            scratch_shapes=[dma((5,))],
        )(*outs)
        return tuple(a.reshape(1, length, width) for a in outs) + (grad_gain.reshape(width),)

    split = P("dp", "seq", "tensor")
    return jax.shard_map(
        shards,
        mesh=mesh,
        in_specs=(split, split, split, P("tensor"), split, P("dp", "seq")),
        out_specs=(split, split, split, split, P("tensor")),
        check_vma=False,
    )
```

```python
import functools

import jax
import jax.numpy as jnp
from jax import lax
from jax.experimental import pallas as pl
from jax.experimental.pallas import tpu as pltpu
from jax.sharding import PartitionSpec as P

DH = 128
BLK = 64
CH = 2048
EPS = 1e-05
CUTS = 2

MESH = pl.DeviceIdType.MESH
F32 = jnp.float32
BF16 = jnp.bfloat16


def dot(a, b, over_a, over_b):
    return lax.dot_general(a, b, (((over_a,), (over_b,)), ((), ())), preferred_element_type=F32)


def kernel(
    sizes, off_hbm, gain_hbm, q_hbm, k_hbm, v_hbm, g_hbm,
    out_ref, gq_ref, gk_ref, gv_ref, gg_ref,
    off_ref, gain_ref, q_ref, k_ref, v_ref, g_ref,
    allow_ref, head_ref, tail_ref, wts_ref, att_ref, pre_ref, pk_ref, pv_ref, sq_ref, raw_ref,
    fsend, frecv, bsend, brecv, stats, gain_own, gain_come, gain_dp, gain_all,
    in_sem, fs_sem, fr_sem, bs_sem, br_sem, ss_sem, sr_sem, left_sem, dp_sem, right_sem,
):
    n_dp, n_seq, n_ten = sizes
    length, width = q_ref.shape
    heads = width // DH
    rows = DH // CUTS
    place = lax.axis_index("seq")
    ten = lax.axis_index("tensor")
    mine = lax.axis_index("dp")
    first, last = place == 0, place == n_seq - 1

    loads = [
        pltpu.make_async_copy(src, dst, in_sem.at[i])
        for i, (src, dst) in enumerate(
            (
                (off_hbm, off_ref), (k_hbm, k_ref), (v_hbm, v_ref),
                (q_hbm, q_ref), (g_hbm, g_ref), (gain_hbm, gain_ref),
            )
        )
    ]
    for load in loads:
        load.start()

    barrier = pltpu.get_barrier_semaphore()

    def greet(device):
        pl.semaphore_signal(barrier, inc=1, device_id=device, device_id_type=MESH)

    @pl.when(jnp.logical_not(last))
    def _():
        greet({"seq": place + 1})

    @pl.when(jnp.logical_not(first))
    def _():
        greet({"seq": place - 1})

    for turn in range(1, n_ten):
        greet({"tensor": lax.rem(ten + turn, n_ten)})
    for turn in range(1, n_dp):
        greet({"dp": lax.rem(mine + turn, n_dp)})
    greeted = n_ten - 1 + n_dp - 1 + jnp.where(last, 0, 1) + jnp.where(first, 0, 1)

    def cols(h):
        return pl.ds(h * DH if isinstance(h, int) else pl.multiple_of(h * DH, DH), DH)

    def piece(part):
        return pl.ds(part * rows, rows)

    def forward(h, part):
        return pltpu.make_async_remote_copy(
            src_ref=fsend.at[h, piece(part)], dst_ref=frecv.at[h, piece(part)],
            send_sem=fs_sem.at[h, part], recv_sem=fr_sem.at[h, part],
            device_id={"seq": place + 1}, device_id_type=MESH,
        )

    def backward(h, part):
        return pltpu.make_async_remote_copy(
            src_ref=bsend.at[h, piece(part)], dst_ref=brecv.at[h, piece(part)],
            send_sem=bs_sem.at[h, part], recv_sem=br_sem.at[h, part],
            device_id={"seq": place - 1}, device_id_type=MESH,
        )

    def each_head(body):
        def step(h, carry):
            body(h)
            return carry

        lax.fori_loop(0, heads, step, 0)

    loads[0].wait()
    starts_at = []
    starts = jnp.int32(0)
    for j in range(off_ref.shape[1]):
        offset = off_ref[0, j]
        starts_at.append(jnp.where(offset < BLK, j * BLK + offset, length))
        starts = starts + jnp.where(offset < BLK, 1, 0)

    def labels(positions):
        total = jnp.zeros(positions.shape, jnp.int32)
        for at in starts_at:
            total = total + jnp.where(positions >= at, 1, 0)
        return total

    label = labels(lax.broadcasted_iota(jnp.int32, (length, DH), 0))
    head_ref[...] = jnp.where(label == 0, 1.0, 0.0).astype(BF16)
    tail_ref[...] = jnp.where(label == starts, 1.0, 0.0).astype(BF16)

    def passed(own, come):
        keep = jnp.full(come.shape, starts, jnp.int32) == 0
        return own + jnp.where(keep, come, 0.0)

    loads[1].wait()
    loads[2].wait()

    def tail(h):
        fsend[h] = dot(k_ref[:, cols(h)] * tail_ref[...], v_ref[:, cols(h)], 0, 0)

    def launch(h):
        @pl.when(first & (n_seq > 1))
        def _():
            for part in range(CUTS):
                forward(h, part).start()

    tail(0)
    pl.semaphore_wait(barrier, greeted)
    launch(0)

    def tails(h, carry):
        tail(h)
        launch(h)
        return carry

    lax.fori_loop(1, heads, tails, 0)

    rows_at = lax.broadcasted_iota(jnp.int32, (length, length), 0)
    cols_at = lax.broadcasted_iota(jnp.int32, (length, length), 1)
    allow_ref[...] = jnp.where(
        (labels(rows_at) == labels(cols_at)) & (cols_at <= rows_at), 1.0, 0.0
    )

    @pl.when(first)
    def _():
        frecv[...] = jnp.zeros_like(frecv)

    @pl.when(last)
    def _():
        brecv[...] = jnp.zeros_like(brecv)

    sq_ref[...] = jnp.zeros_like(sq_ref)
    raw_ref[...] = jnp.zeros_like(raw_ref)
    for load in loads[3:]:
        load.wait()

    def relay_right(h, part):
        @pl.when(jnp.logical_not(first))
        def _():
            forward(h, part).wait_recv()

            @pl.when(jnp.logical_not(last))
            def _():
                fsend[h, piece(part)] = passed(fsend[h, piece(part)], frecv[h, piece(part)])
                forward(h, part).start()

    def attend(h):
        scores = dot(q_ref[:, cols(h)], k_ref[:, cols(h)], 1, 1)
        wts_ref[h] = (scores * allow_ref[...]).astype(BF16)
        att_ref[:, cols(h)] = dot(wts_ref[h], v_ref[:, cols(h)], 1, 0)

    def add_carried(h):
        attended = att_ref[:, cols(h)] + dot(
            q_ref[:, cols(h)] * head_ref[...], frecv[h].astype(BF16), 1, 0
        )
        att_ref[:, cols(h)] = attended
        sq_ref[...] = sq_ref[...] + attended * attended
        raw_ref[...] = raw_ref[...] + gain_ref[:, cols(h)] * g_ref[:, cols(h)].astype(F32) * attended

    def staggered(ahead, local, relay, finish):
        def before(h, carry):
            local(h)
            return carry

        lax.fori_loop(0, ahead, before, 0)

        def step(h):
            relay(h, 0)

            @pl.when(h + ahead < heads)
            def _():
                local(h + ahead)

            for part in range(1, CUTS):
                relay(h, part)
            finish(h)

        each_head(step)

    ahead = jnp.where(first | last, heads, jnp.minimum(place, heads))
    staggered(ahead, attend, relay_right, add_carried)

    stats[ten, 0:1, :] = jnp.sum(sq_ref[...].T, axis=0, keepdims=True)
    stats[ten, 1:2, :] = jnp.sum(raw_ref[...].T, axis=0, keepdims=True)

    def exchange(turn, slot):
        return pltpu.make_async_remote_copy(
            src_ref=stats.at[slot], dst_ref=stats.at[slot],
            send_sem=ss_sem.at[turn], recv_sem=sr_sem.at[slot],
            device_id={"tensor": lax.rem(ten + turn, n_ten)}, device_id_type=MESH,
        )

    for turn in range(1, n_ten):
        exchange(turn, ten).start()
    for turn in range(1, n_ten):
        exchange(turn, lax.rem(ten + turn, n_ten)).wait_recv()
    totals = stats[0]
    for t in range(1, n_ten):
        totals = totals + stats[t]
    inverse = lax.rsqrt(totals[0:1, :] / CH + EPS)
    slope = inverse * inverse * (totals[1:2, :] / CH)
    sq_ref[...] = jnp.broadcast_to(inverse, (DH, length)).T
    raw_ref[...] = jnp.broadcast_to(slope, (DH, length)).T

    def before_norm(h):
        upstream = g_ref[:, cols(h)].astype(F32)
        pre = sq_ref[...] * (gain_ref[:, cols(h)] * upstream - att_ref[:, cols(h)] * raw_ref[...])
        pre = pre.astype(BF16)
        pre_ref[:, cols(h)] = pre
        bsend[h] = dot(q_ref[:, cols(h)] * head_ref[...], pre, 0, 0)

        @pl.when(last & (n_seq > 1))
        def _():
            for part in range(CUTS):
                backward(h, part).start()

    each_head(before_norm)

    def after_norm(h):
        normed = att_ref[:, cols(h)] * sq_ref[...]
        out_ref[:, cols(h)] = (gain_ref[:, cols(h)] * normed).astype(BF16)
        gain_own[:, cols(h)] = jnp.sum(
            g_ref[:, cols(h)].astype(F32) * normed, axis=0, keepdims=True
        )

    for h in range(heads):
        after_norm(h)

    gain_left = pltpu.make_async_remote_copy(
        src_ref=gain_own, dst_ref=gain_come, send_sem=left_sem.at[0], recv_sem=left_sem.at[1],
        device_id={"seq": place - 1}, device_id_type=MESH,
    )
    gain_right = pltpu.make_async_remote_copy(
        src_ref=gain_all, dst_ref=gain_all, send_sem=right_sem.at[0], recv_sem=right_sem.at[1],
        device_id={"seq": place + 1}, device_id_type=MESH,
    )

    def across(turn, slot):
        return pltpu.make_async_remote_copy(
            src_ref=gain_dp.at[slot], dst_ref=gain_dp.at[slot],
            send_sem=dp_sem.at[0, turn], recv_sem=dp_sem.at[1, slot],
            device_id={"dp": lax.rem(mine + turn, n_dp)}, device_id_type=MESH,
        )

    def gain_relay():
        @pl.when(jnp.logical_not(last))
        def _():
            gain_left.wait_recv()
            gain_own[...] = gain_own[...] + gain_come[...]

        @pl.when(jnp.logical_not(first))
        def _():
            gain_left.start()

        @pl.when(first)
        def _():
            gain_dp[mine] = gain_own[...]
            for turn in range(1, n_dp):
                across(turn, mine).start()

    def gain_total():
        @pl.when(first)
        def _():
            for turn in range(1, n_dp):
                across(turn, lax.rem(mine + turn, n_dp)).wait_recv()
            total = gain_dp[0]
            for i in range(1, n_dp):
                total = total + gain_dp[i]
            gain_all[...] = total

        @pl.when(jnp.logical_not(first))
        def _():
            gain_right.wait_recv()

        @pl.when(jnp.logical_not(last))
        def _():
            gain_right.start()

        gg_ref[...] = gain_all[...]

    @pl.when(last)
    def _():
        gain_relay()

    def relay_left(h, part):
        @pl.when(jnp.logical_not(last))
        def _():
            backward(h, part).wait_recv()

            @pl.when(jnp.logical_not(first))
            def _():
                bsend[h, piece(part)] = passed(bsend[h, piece(part)], brecv[h, piece(part)])
                backward(h, part).start()

    def local_grads(h):
        pre = pre_ref[:, cols(h)]
        grad_weights = (dot(pre, v_ref[:, cols(h)], 1, 1) * allow_ref[...]).astype(BF16)
        gq = dot(grad_weights, k_ref[:, cols(h)], 1, 0)
        gq = gq + dot(pre * head_ref[...], frecv[h].astype(BF16), 1, 1)
        gq_ref[:, cols(h)] = gq.astype(BF16)
        pk_ref[:, cols(h)] = dot(grad_weights, q_ref[:, cols(h)], 0, 0)

        pv_ref[:, cols(h)] = dot(wts_ref[h], pre, 0, 0)

    def finish(h):
        later = brecv[h].astype(BF16)
        gk = pk_ref[:, cols(h)] + dot(v_ref[:, cols(h)] * tail_ref[...], later, 1, 1)
        gk_ref[:, cols(h)] = gk.astype(BF16)
        gv = pv_ref[:, cols(h)] + dot(k_ref[:, cols(h)] * tail_ref[...], later, 1, 0)
        gv_ref[:, cols(h)] = gv.astype(BF16)

        @pl.when((h == jnp.where(first, heads - 2, heads // 2 - 1)) & jnp.logical_not(last))
        def _():
            gain_relay()

    ahead = jnp.where(last, heads, jnp.minimum(n_seq - place, heads))
    staggered(ahead, local_grads, relay_left, finish)
    gain_total()

    @pl.when(first)
    def _():
        for turn in range(1, n_dp):
            across(turn, mine).wait_send()

    for turn in range(1, n_ten):
        exchange(turn, ten).wait_send()

    @pl.when(jnp.logical_not(last))
    def _():
        for h in range(heads):
            for part in range(CUTS):
                forward(h, part).wait_send()
        gain_right.wait_send()

    @pl.when(jnp.logical_not(first))
    def _():
        for h in range(heads):
            for part in range(CUTS):
                backward(h, part).wait_send()
        gain_left.wait_send()


def hand_out(*refs):
    count = len(refs) // 2
    copies = [
        pltpu.make_async_copy(refs[i], refs[count + i], refs[-1].at[i]) for i in range(count)
    ]
    for copy in copies:
        copy.start()
    for copy in copies:
        copy.wait()


def solution(mesh):
    sizes = (mesh.shape["dp"], mesh.shape["seq"], mesh.shape["tensor"])

    def shards(query, key_rows, value, gain, grad_out, start_offset):
        _, length, width = query.shape
        heads = width // DH
        hbm = pl.BlockSpec(memory_space=pltpu.HBM)
        vmem = pl.BlockSpec(memory_space=pltpu.VMEM)
        rows = jax.ShapeDtypeStruct((length, width), BF16)
        shapes = (rows,) * 4 + (jax.ShapeDtypeStruct((1, width), F32),)
        dma = pltpu.SemaphoreType.DMA
        flat = lambda a: a.reshape(length, width)
        outs = pl.pallas_call(
            functools.partial(kernel, sizes),
            out_shape=tuple(pltpu.VMEM(a.shape, a.dtype) for a in shapes),
            in_specs=[hbm] * 6,
            out_specs=(vmem,) * 5,
            scratch_shapes=[pltpu.SMEM(start_offset.shape, jnp.int32), pltpu.VMEM((1, width), F32)]
            + [pltpu.VMEM((length, width), BF16)] * 4
            + [
                pltpu.VMEM((length, length), F32),
                pltpu.VMEM((length, DH), BF16),
                pltpu.VMEM((length, DH), BF16),
                pltpu.VMEM((heads, length, length), BF16),
                pltpu.VMEM((length, width), F32),
                pltpu.VMEM((length, width), BF16),
                pltpu.VMEM((length, width), F32),
                pltpu.VMEM((length, width), F32),
                pltpu.VMEM((length, DH), F32),
                pltpu.VMEM((length, DH), F32),
            ]
            + [pltpu.VMEM((heads, DH, DH), F32)] * 4
            + [pltpu.VMEM((sizes[2], 2, length), F32), pltpu.VMEM((1, width), F32), pltpu.VMEM((1, width), F32)]
            + [pltpu.VMEM((sizes[0], 1, width), F32), pltpu.VMEM((1, width), F32)]
            + [dma((6,))] + [dma((heads, CUTS))] * 4
            + [dma((sizes[2],)), dma((sizes[2],)), dma((2,)), dma((2, sizes[0])), dma((2,))],
            compiler_params=pltpu.CompilerParams(
                collective_id=0, has_side_effects=True, vmem_limit_bytes=61 * 1024 * 1024
            ),
        )(start_offset, gain.reshape(1, width), flat(query), flat(key_rows), flat(value), flat(grad_out))
        *outs, grad_gain = pl.pallas_call(
            hand_out,
            out_shape=shapes,
            in_specs=[vmem] * 5,
            out_specs=(hbm,) * 5,
            scratch_shapes=[dma((5,))],
            compiler_params=pltpu.CompilerParams(vmem_limit_bytes=8 * 1024 * 1024),
        )(*outs)
        return tuple(a.reshape(1, length, width) for a in outs) + (grad_gain.reshape(width),)

    split = P("dp", "seq", "tensor")
    return jax.shard_map(
        shards,
        mesh=mesh,
        in_specs=(split, split, split, P("tensor"), split, P("dp", "seq")),
        out_specs=(split, split, split, split, P("tensor")),
        check_vma=False,
    )
```

```python
import functools

import jax
import jax.numpy as jnp
from jax import lax
from jax.experimental import pallas as pl
from jax.experimental.pallas import tpu as pltpu
from jax.sharding import PartitionSpec as P

DH = 128
BLK = 64
CH = 2048
EPS = 1e-05
CUTS = 4

MESH = pl.DeviceIdType.MESH
F32 = jnp.float32
BF16 = jnp.bfloat16


def dot(a, b, over_a, over_b):
    return lax.dot_general(a, b, (((over_a,), (over_b,)), ((), ())), preferred_element_type=F32)


def kernel(
    sizes, off_hbm, gain_hbm, q_hbm, k_hbm, v_hbm, g_hbm,
    out_ref, gq_ref, gk_ref, gv_ref, gg_ref,
    off_ref, gain_ref, q_ref, k_ref, v_ref, g_ref,
    allow_ref, head_ref, tail_ref, wts_ref, att_ref, pre_ref, pk_ref, pv_ref, sq_ref, raw_ref,
    fsend, frecv, bsend, brecv, stats, gain_own, gain_come, gain_dp, gain_all,
    in_sem, fs_sem, fr_sem, bs_sem, br_sem, ss_sem, sr_sem, left_sem, dp_sem, right_sem,
):
    n_dp, n_seq, n_ten = sizes
    length, width = q_ref.shape
    heads = width // DH
    rows = DH // CUTS
    place = lax.axis_index("seq")
    ten = lax.axis_index("tensor")
    mine = lax.axis_index("dp")
    first, last = place == 0, place == n_seq - 1

    loads = [
        pltpu.make_async_copy(src, dst, in_sem.at[i])
        for i, (src, dst) in enumerate(
            (
                (off_hbm, off_ref), (k_hbm, k_ref), (v_hbm, v_ref),
                (q_hbm, q_ref), (g_hbm, g_ref), (gain_hbm, gain_ref),
            )
        )
    ]
    for load in loads:
        load.start()

    barrier = pltpu.get_barrier_semaphore()

    def greet(device):
        pl.semaphore_signal(barrier, inc=1, device_id=device, device_id_type=MESH)

    @pl.when(jnp.logical_not(last))
    def _():
        greet({"seq": place + 1})

    @pl.when(jnp.logical_not(first))
    def _():
        greet({"seq": place - 1})

    for turn in range(1, n_ten):
        greet({"tensor": lax.rem(ten + turn, n_ten)})
    for turn in range(1, n_dp):
        greet({"dp": lax.rem(mine + turn, n_dp)})
    greeted = n_ten - 1 + n_dp - 1 + jnp.where(last, 0, 1) + jnp.where(first, 0, 1)

    def cols(h):
        return pl.ds(h * DH if isinstance(h, int) else pl.multiple_of(h * DH, DH), DH)

    def piece(part):
        return pl.ds(part * rows, rows)

    def forward(h, part):
        return pltpu.make_async_remote_copy(
            src_ref=fsend.at[h, piece(part)], dst_ref=frecv.at[h, piece(part)],
            send_sem=fs_sem.at[h, part], recv_sem=fr_sem.at[h, part],
            device_id={"seq": place + 1}, device_id_type=MESH,
        )

    def backward(h, part):
        return pltpu.make_async_remote_copy(
            src_ref=bsend.at[h, piece(part)], dst_ref=brecv.at[h, piece(part)],
            send_sem=bs_sem.at[h, part], recv_sem=br_sem.at[h, part],
            device_id={"seq": place - 1}, device_id_type=MESH,
        )

    def each_head(body):
        def step(h, carry):
            body(h)
            return carry

        lax.fori_loop(0, heads, step, 0)

    loads[0].wait()
    starts_at = []
    starts = jnp.int32(0)
    for j in range(off_ref.shape[1]):
        offset = off_ref[0, j]
        starts_at.append(jnp.where(offset < BLK, j * BLK + offset, length))
        starts = starts + jnp.where(offset < BLK, 1, 0)

    def labels(positions):
        total = jnp.zeros(positions.shape, jnp.int32)
        for at in starts_at:
            total = total + jnp.where(positions >= at, 1, 0)
        return total

    label = labels(lax.broadcasted_iota(jnp.int32, (length, DH), 0))
    head_ref[...] = jnp.where(label == 0, 1.0, 0.0).astype(BF16)
    tail_ref[...] = jnp.where(label == starts, 1.0, 0.0).astype(BF16)

    def passed(own, come):
        keep = jnp.full(come.shape, starts, jnp.int32) == 0
        return own + jnp.where(keep, come, 0.0)

    loads[1].wait()
    loads[2].wait()

    def tail(h):
        fsend[h] = dot(k_ref[:, cols(h)] * tail_ref[...], v_ref[:, cols(h)], 0, 0)

    def launch(h):
        @pl.when(first & (n_seq > 1))
        def _():
            for part in range(CUTS):
                forward(h, part).start()

    tail(0)
    pl.semaphore_wait(barrier, greeted)
    launch(0)

    def tails(h, carry):
        tail(h)
        launch(h)
        return carry

    lax.fori_loop(1, heads, tails, 0)

    rows_at = lax.broadcasted_iota(jnp.int32, (length, length), 0)
    cols_at = lax.broadcasted_iota(jnp.int32, (length, length), 1)
    allow_ref[...] = jnp.where(
        (labels(rows_at) == labels(cols_at)) & (cols_at <= rows_at), 1.0, 0.0
    )

    @pl.when(first)
    def _():
        frecv[...] = jnp.zeros_like(frecv)

    @pl.when(last)
    def _():
        brecv[...] = jnp.zeros_like(brecv)

    sq_ref[...] = jnp.zeros_like(sq_ref)
    raw_ref[...] = jnp.zeros_like(raw_ref)
    for load in loads[3:]:
        load.wait()

    def relay_right(h, part):
        @pl.when(jnp.logical_not(first))
        def _():
            forward(h, part).wait_recv()

            @pl.when(jnp.logical_not(last))
            def _():
                fsend[h, piece(part)] = passed(fsend[h, piece(part)], frecv[h, piece(part)])
                forward(h, part).start()

    def attend(h):
        scores = dot(q_ref[:, cols(h)], k_ref[:, cols(h)], 1, 1)
        wts_ref[h] = (scores * allow_ref[...]).astype(BF16)
        att_ref[:, cols(h)] = dot(wts_ref[h], v_ref[:, cols(h)], 1, 0)

    def add_carried(h):
        attended = att_ref[:, cols(h)] + dot(
            q_ref[:, cols(h)] * head_ref[...], frecv[h].astype(BF16), 1, 0
        )
        att_ref[:, cols(h)] = attended
        sq_ref[...] = sq_ref[...] + attended * attended
        raw_ref[...] = raw_ref[...] + gain_ref[:, cols(h)] * g_ref[:, cols(h)].astype(F32) * attended

    def staggered(ahead, local, relay, finish, passed_on):
        def before(h, carry):
            local(h)
            return carry

        lax.fori_loop(0, ahead, before, 0)

        @pl.when(first | last)
        def _():
            def step(h):
                for part in range(CUTS):
                    relay(h, part)
                finish(h)

            each_head(step)

        @pl.when(jnp.logical_not(first | last))
        def _():
            def step(h):
                for part in range(CUTS):
                    relay(h, part)

            each_head(step)
            passed_on()

            def rest(h):
                @pl.when(h >= ahead)
                def _():
                    local(h)

                finish(h)

            each_head(rest)

    ahead = jnp.where(first | last | (place > 1), heads, 1)
    staggered(ahead, attend, relay_right, add_carried, lambda: None)

    stats[ten, 0:1, :] = jnp.sum(sq_ref[...].T, axis=0, keepdims=True)
    stats[ten, 1:2, :] = jnp.sum(raw_ref[...].T, axis=0, keepdims=True)

    def exchange(turn, slot):
        return pltpu.make_async_remote_copy(
            src_ref=stats.at[slot], dst_ref=stats.at[slot],
            send_sem=ss_sem.at[turn], recv_sem=sr_sem.at[slot],
            device_id={"tensor": lax.rem(ten + turn, n_ten)}, device_id_type=MESH,
        )

    for turn in range(1, n_ten):
        exchange(turn, ten).start()
    for turn in range(1, n_ten):
        exchange(turn, lax.rem(ten + turn, n_ten)).wait_recv()
    totals = stats[0]
    for t in range(1, n_ten):
        totals = totals + stats[t]
    inverse = lax.rsqrt(totals[0:1, :] / CH + EPS)
    slope = inverse * inverse * (totals[1:2, :] / CH)
    sq_ref[...] = jnp.broadcast_to(inverse, (DH, length)).T
    raw_ref[...] = jnp.broadcast_to(slope, (DH, length)).T

    def before_norm(h):
        upstream = g_ref[:, cols(h)].astype(F32)
        pre = sq_ref[...] * (gain_ref[:, cols(h)] * upstream - att_ref[:, cols(h)] * raw_ref[...])
        pre = pre.astype(BF16)
        pre_ref[:, cols(h)] = pre
        bsend[h] = dot(q_ref[:, cols(h)] * head_ref[...], pre, 0, 0)

        @pl.when(last & (n_seq > 1))
        def _():
            for part in range(CUTS):
                backward(h, part).start()

    each_head(before_norm)

    def after_norm(h):
        normed = att_ref[:, cols(h)] * sq_ref[...]
        out_ref[:, cols(h)] = (gain_ref[:, cols(h)] * normed).astype(BF16)
        gain_own[:, cols(h)] = jnp.sum(
            g_ref[:, cols(h)].astype(F32) * normed, axis=0, keepdims=True
        )

    for h in range(heads):
        after_norm(h)

    gain_right = pltpu.make_async_remote_copy(
        src_ref=gain_own, dst_ref=gain_come, send_sem=right_sem.at[0], recv_sem=right_sem.at[1],
        device_id={"seq": place + 1}, device_id_type=MESH,
    )
    gain_left = pltpu.make_async_remote_copy(
        src_ref=gain_all, dst_ref=gain_all, send_sem=left_sem.at[0], recv_sem=left_sem.at[1],
        device_id={"seq": place - 1}, device_id_type=MESH,
    )

    def across(turn, slot):
        return pltpu.make_async_remote_copy(
            src_ref=gain_dp.at[slot], dst_ref=gain_dp.at[slot],
            send_sem=dp_sem.at[0, turn], recv_sem=dp_sem.at[1, slot],
            device_id={"dp": lax.rem(mine + turn, n_dp)}, device_id_type=MESH,
        )

    def hand_gain_on():
        @pl.when(jnp.logical_not(last))
        def _():
            gain_left.wait_recv()

        @pl.when(jnp.logical_not(first))
        def _():
            gain_left.start()

        gg_ref[...] = gain_all[...]

    @pl.when(jnp.logical_not(first))
    def _():
        gain_right.wait_recv()
        gain_own[...] = gain_own[...] + gain_come[...]

    @pl.when(jnp.logical_not(last))
    def _():
        gain_right.start()

    @pl.when(last)
    def _():
        gain_dp[mine] = gain_own[...]
        for turn in range(1, n_dp):
            across(turn, mine).start()
        for turn in range(1, n_dp):
            across(turn, lax.rem(mine + turn, n_dp)).wait_recv()
        total = gain_dp[0]
        for i in range(1, n_dp):
            total = total + gain_dp[i]
        gain_all[...] = total
        hand_gain_on()

    def relay_left(h, part):
        @pl.when(jnp.logical_not(last))
        def _():
            backward(h, part).wait_recv()

            @pl.when(jnp.logical_not(first))
            def _():
                bsend[h, piece(part)] = passed(bsend[h, piece(part)], brecv[h, piece(part)])
                backward(h, part).start()

    def local_grads(h):
        pre = pre_ref[:, cols(h)]
        grad_weights = (dot(pre, v_ref[:, cols(h)], 1, 1) * allow_ref[...]).astype(BF16)
        gq = dot(grad_weights, k_ref[:, cols(h)], 1, 0)
        gq = gq + dot(pre * head_ref[...], frecv[h].astype(BF16), 1, 1)
        gq_ref[:, cols(h)] = gq.astype(BF16)
        pk_ref[:, cols(h)] = dot(grad_weights, q_ref[:, cols(h)], 0, 0)

        pv_ref[:, cols(h)] = dot(wts_ref[h], pre, 0, 0)

    def finish(h):
        later = brecv[h].astype(BF16)
        gk = pk_ref[:, cols(h)] + dot(v_ref[:, cols(h)] * tail_ref[...], later, 1, 1)
        gk_ref[:, cols(h)] = gk.astype(BF16)
        gv = pv_ref[:, cols(h)] + dot(k_ref[:, cols(h)] * tail_ref[...], later, 1, 0)
        gv_ref[:, cols(h)] = gv.astype(BF16)

    ahead = jnp.where(last, heads, jnp.minimum(n_seq - place, heads))
    staggered(ahead, local_grads, relay_left, finish, hand_gain_on)

    @pl.when(first & (n_seq > 1))
    def _():
        hand_gain_on()

    @pl.when(last)
    def _():
        for turn in range(1, n_dp):
            across(turn, mine).wait_send()

    for turn in range(1, n_ten):
        exchange(turn, ten).wait_send()

    @pl.when(jnp.logical_not(last))
    def _():
        for h in range(heads):
            for part in range(CUTS):
                forward(h, part).wait_send()
        gain_right.wait_send()

    @pl.when(jnp.logical_not(first))
    def _():
        for h in range(heads):
            for part in range(CUTS):
                backward(h, part).wait_send()
        gain_left.wait_send()


def hand_out(*refs):
    count = len(refs) // 2
    copies = [
        pltpu.make_async_copy(refs[i], refs[count + i], refs[-1].at[i]) for i in range(count)
    ]
    for copy in copies:
        copy.start()
    for copy in copies:
        copy.wait()


def solution(mesh):
    sizes = (mesh.shape["dp"], mesh.shape["seq"], mesh.shape["tensor"])

    def shards(query, key_rows, value, gain, grad_out, start_offset):
        _, length, width = query.shape
        heads = width // DH
        hbm = pl.BlockSpec(memory_space=pltpu.HBM)
        vmem = pl.BlockSpec(memory_space=pltpu.VMEM)
        rows = jax.ShapeDtypeStruct((length, width), BF16)
        shapes = (rows,) * 4 + (jax.ShapeDtypeStruct((1, width), F32),)
        dma = pltpu.SemaphoreType.DMA
        flat = lambda a: a.reshape(length, width)
        outs = pl.pallas_call(
            functools.partial(kernel, sizes),
            out_shape=tuple(pltpu.VMEM(a.shape, a.dtype) for a in shapes),
            in_specs=[hbm] * 6,
            out_specs=(vmem,) * 5,
            scratch_shapes=[pltpu.SMEM(start_offset.shape, jnp.int32), pltpu.VMEM((1, width), F32)]
            + [pltpu.VMEM((length, width), BF16)] * 4
            + [
                pltpu.VMEM((length, length), F32),
                pltpu.VMEM((length, DH), BF16),
                pltpu.VMEM((length, DH), BF16),
                pltpu.VMEM((heads, length, length), BF16),
                pltpu.VMEM((length, width), F32),
                pltpu.VMEM((length, width), BF16),
                pltpu.VMEM((length, width), F32),
                pltpu.VMEM((length, width), F32),
                pltpu.VMEM((length, DH), F32),
                pltpu.VMEM((length, DH), F32),
            ]
            + [pltpu.VMEM((heads, DH, DH), F32)] * 4
            + [pltpu.VMEM((sizes[2], 2, length), F32), pltpu.VMEM((1, width), F32), pltpu.VMEM((1, width), F32)]
            + [pltpu.VMEM((sizes[0], 1, width), F32), pltpu.VMEM((1, width), F32)]
            + [dma((6,))] + [dma((heads, CUTS))] * 4
            + [dma((sizes[2],)), dma((sizes[2],)), dma((2,)), dma((2, sizes[0])), dma((2,))],
            compiler_params=pltpu.CompilerParams(
                collective_id=0, has_side_effects=True, vmem_limit_bytes=61 * 1024 * 1024
            ),
        )(start_offset, gain.reshape(1, width), flat(query), flat(key_rows), flat(value), flat(grad_out))
        *outs, grad_gain = pl.pallas_call(
            hand_out,
            out_shape=shapes,
            in_specs=[vmem] * 5,
            out_specs=(hbm,) * 5,
            scratch_shapes=[dma((5,))],
            compiler_params=pltpu.CompilerParams(vmem_limit_bytes=8 * 1024 * 1024),
        )(*outs)
        return tuple(a.reshape(1, length, width) for a in outs) + (grad_gain.reshape(width),)

    split = P("dp", "seq", "tensor")
    return jax.shard_map(
        shards,
        mesh=mesh,
        in_specs=(split, split, split, P("tensor"), split, P("dp", "seq")),
        out_specs=(split, split, split, split, P("tensor")),
        check_vma=False,
    )
```

```python
import functools

import jax
import jax.numpy as jnp
from jax import lax
from jax.experimental import pallas as pl
from jax.experimental.pallas import tpu as pltpu
from jax.sharding import PartitionSpec as P

DH = 128
BLK = 64
CH = 2048
EPS = 1e-05
CUTS = 4

MESH = pl.DeviceIdType.MESH
F32 = jnp.float32
BF16 = jnp.bfloat16


def dot(a, b, over_a, over_b):
    return lax.dot_general(a, b, (((over_a,), (over_b,)), ((), ())), preferred_element_type=F32)


def kernel(
    sizes, off_hbm, gain_hbm, q_hbm, k_hbm, v_hbm, g_hbm,
    out_ref, gq_ref, gk_ref, gv_ref, gg_ref,
    off_ref, gain_ref, q_ref, k_ref, v_ref, g_ref,
    allow_ref, head_ref, tail_ref, wts_ref, att_ref, pre_ref, pk_ref, pv_ref, sq_ref, raw_ref,
    fsend, frecv, bsend, brecv, stats, gain_own, gain_come, gain_dp, gain_all,
    in_sem, fs_sem, fr_sem, bs_sem, br_sem, ss_sem, sr_sem, left_sem, dp_sem, right_sem,
):
    n_dp, n_seq, n_ten = sizes
    length, width = q_ref.shape
    heads = width // DH
    rows = DH // CUTS
    place = lax.axis_index("seq")
    ten = lax.axis_index("tensor")
    mine = lax.axis_index("dp")
    first, last = place == 0, place == n_seq - 1

    loads = [
        pltpu.make_async_copy(src, dst, in_sem.at[i])
        for i, (src, dst) in enumerate(
            (
                (off_hbm, off_ref), (k_hbm, k_ref), (v_hbm, v_ref),
                (q_hbm, q_ref), (g_hbm, g_ref), (gain_hbm, gain_ref),
            )
        )
    ]
    for load in loads:
        load.start()

    barrier = pltpu.get_barrier_semaphore()

    def greet(device):
        pl.semaphore_signal(barrier, inc=1, device_id=device, device_id_type=MESH)

    @pl.when(jnp.logical_not(last))
    def _():
        greet({"seq": place + 1})

    @pl.when(jnp.logical_not(first))
    def _():
        greet({"seq": place - 1})

    for turn in range(1, n_ten):
        greet({"tensor": lax.rem(ten + turn, n_ten)})
    for turn in range(1, n_dp):
        greet({"dp": lax.rem(mine + turn, n_dp)})
    greeted = n_ten - 1 + n_dp - 1 + jnp.where(last, 0, 1) + jnp.where(first, 0, 1)

    def cols(h):
        return pl.ds(h * DH if isinstance(h, int) else pl.multiple_of(h * DH, DH), DH)

    def piece(part):
        return pl.ds(part * rows, rows)

    def forward(h, part):
        return pltpu.make_async_remote_copy(
            src_ref=fsend.at[h, piece(part)], dst_ref=frecv.at[h, piece(part)],
            send_sem=fs_sem.at[h, part], recv_sem=fr_sem.at[h, part],
            device_id={"seq": place + 1}, device_id_type=MESH,
        )

    def backward(h, part):
        return pltpu.make_async_remote_copy(
            src_ref=bsend.at[h, piece(part)], dst_ref=brecv.at[h, piece(part)],
            send_sem=bs_sem.at[h, part], recv_sem=br_sem.at[h, part],
            device_id={"seq": place - 1}, device_id_type=MESH,
        )

    def each_head(body):
        def step(h, carry):
            body(h)
            return carry

        lax.fori_loop(0, heads, step, 0)

    loads[0].wait()
    starts_at = []
    starts = jnp.int32(0)
    for j in range(off_ref.shape[1]):
        offset = off_ref[0, j]
        starts_at.append(jnp.where(offset < BLK, j * BLK + offset, length))
        starts = starts + jnp.where(offset < BLK, 1, 0)

    def labels(positions):
        total = jnp.zeros(positions.shape, jnp.int32)
        for at in starts_at:
            total = total + jnp.where(positions >= at, 1, 0)
        return total

    label = labels(lax.broadcasted_iota(jnp.int32, (length, DH), 0))
    head_ref[...] = jnp.where(label == 0, 1.0, 0.0).astype(BF16)
    tail_ref[...] = jnp.where(label == starts, 1.0, 0.0).astype(BF16)

    def passed(own, come):
        keep = jnp.full(come.shape, starts, jnp.int32) == 0
        return own + jnp.where(keep, come, 0.0)

    loads[1].wait()
    loads[2].wait()

    def tail(h):
        fsend[h] = dot(k_ref[:, cols(h)] * tail_ref[...], v_ref[:, cols(h)], 0, 0)

    def launch(h):
        @pl.when(first & (n_seq > 1))
        def _():
            for part in range(CUTS):
                forward(h, part).start()

    tail(0)
    pl.semaphore_wait(barrier, greeted)
    launch(0)

    def tails(h, carry):
        tail(h)
        launch(h)
        return carry

    lax.fori_loop(1, heads, tails, 0)

    rows_at = lax.broadcasted_iota(jnp.int32, (length, length), 0)
    cols_at = lax.broadcasted_iota(jnp.int32, (length, length), 1)
    allow_ref[...] = jnp.where(
        (labels(rows_at) == labels(cols_at)) & (cols_at <= rows_at), 1.0, 0.0
    )

    @pl.when(first)
    def _():
        frecv[...] = jnp.zeros_like(frecv)

    @pl.when(last)
    def _():
        brecv[...] = jnp.zeros_like(brecv)

    sq_ref[...] = jnp.zeros_like(sq_ref)
    raw_ref[...] = jnp.zeros_like(raw_ref)
    for load in loads[3:]:
        load.wait()

    def relay_right(h, part):
        @pl.when(jnp.logical_not(first))
        def _():
            forward(h, part).wait_recv()

            @pl.when(jnp.logical_not(last))
            def _():
                fsend[h, piece(part)] = passed(fsend[h, piece(part)], frecv[h, piece(part)])
                forward(h, part).start()

    def attend(h):
        scores = dot(q_ref[:, cols(h)], k_ref[:, cols(h)], 1, 1)
        wts_ref[h] = (scores * allow_ref[...]).astype(BF16)
        att_ref[:, cols(h)] = dot(wts_ref[h], v_ref[:, cols(h)], 1, 0)

    def add_carried(h):
        attended = att_ref[:, cols(h)] + dot(
            q_ref[:, cols(h)] * head_ref[...], frecv[h].astype(BF16), 1, 0
        )
        att_ref[:, cols(h)] = attended
        sq_ref[...] = sq_ref[...] + attended * attended
        raw_ref[...] = raw_ref[...] + gain_ref[:, cols(h)] * g_ref[:, cols(h)].astype(F32) * attended

    def staggered(ahead, local, relay, finish, passed_on):
        def before(h, carry):
            local(h)
            return carry

        lax.fori_loop(0, ahead, before, 0)

        @pl.when(first | last)
        def _():
            def step(h):
                for part in range(CUTS):
                    relay(h, part)
                finish(h)

            each_head(step)

        @pl.when(jnp.logical_not(first | last))
        def _():
            def step(h):
                for part in range(CUTS):
                    relay(h, part)

            each_head(step)
            passed_on()

            def rest(h):
                @pl.when(h >= ahead)
                def _():
                    local(h)

                finish(h)

            each_head(rest)

    ahead = jnp.where(first | last, heads, jnp.minimum(2 * place - 1, heads))
    staggered(ahead, attend, relay_right, add_carried, lambda: None)

    stats[ten, 0:1, :] = jnp.sum(sq_ref[...].T, axis=0, keepdims=True)
    stats[ten, 1:2, :] = jnp.sum(raw_ref[...].T, axis=0, keepdims=True)

    def exchange(turn, slot):
        return pltpu.make_async_remote_copy(
            src_ref=stats.at[slot], dst_ref=stats.at[slot],
            send_sem=ss_sem.at[turn], recv_sem=sr_sem.at[slot],
            device_id={"tensor": lax.rem(ten + turn, n_ten)}, device_id_type=MESH,
        )

    for turn in range(1, n_ten):
        exchange(turn, ten).start()
    for turn in range(1, n_ten):
        exchange(turn, lax.rem(ten + turn, n_ten)).wait_recv()
    totals = stats[0]
    for t in range(1, n_ten):
        totals = totals + stats[t]
    inverse = lax.rsqrt(totals[0:1, :] / CH + EPS)
    slope = inverse * inverse * (totals[1:2, :] / CH)
    sq_ref[...] = jnp.broadcast_to(inverse, (DH, length)).T
    raw_ref[...] = jnp.broadcast_to(slope, (DH, length)).T

    def before_norm(h):
        upstream = g_ref[:, cols(h)].astype(F32)
        pre = sq_ref[...] * (gain_ref[:, cols(h)] * upstream - att_ref[:, cols(h)] * raw_ref[...])
        pre = pre.astype(BF16)
        pre_ref[:, cols(h)] = pre
        bsend[h] = dot(q_ref[:, cols(h)] * head_ref[...], pre, 0, 0)

        @pl.when(last & (n_seq > 1))
        def _():
            for part in range(CUTS):
                backward(h, part).start()

    each_head(before_norm)

    def after_norm(h):
        normed = att_ref[:, cols(h)] * sq_ref[...]
        out_ref[:, cols(h)] = (gain_ref[:, cols(h)] * normed).astype(BF16)
        gain_own[:, cols(h)] = jnp.sum(
            g_ref[:, cols(h)].astype(F32) * normed, axis=0, keepdims=True
        )

    for h in range(heads):
        after_norm(h)

    gain_right = pltpu.make_async_remote_copy(
        src_ref=gain_own, dst_ref=gain_come, send_sem=right_sem.at[0], recv_sem=right_sem.at[1],
        device_id={"seq": place + 1}, device_id_type=MESH,
    )
    gain_left = pltpu.make_async_remote_copy(
        src_ref=gain_all, dst_ref=gain_all, send_sem=left_sem.at[0], recv_sem=left_sem.at[1],
        device_id={"seq": place - 1}, device_id_type=MESH,
    )

    def across(turn, slot):
        return pltpu.make_async_remote_copy(
            src_ref=gain_dp.at[slot], dst_ref=gain_dp.at[slot],
            send_sem=dp_sem.at[0, turn], recv_sem=dp_sem.at[1, slot],
            device_id={"dp": lax.rem(mine + turn, n_dp)}, device_id_type=MESH,
        )

    def hand_gain_on():
        @pl.when(jnp.logical_not(last))
        def _():
            gain_left.wait_recv()

        @pl.when(jnp.logical_not(first))
        def _():
            gain_left.start()

        gg_ref[...] = gain_all[...]

    @pl.when(jnp.logical_not(first))
    def _():
        gain_right.wait_recv()
        gain_own[...] = gain_own[...] + gain_come[...]

    @pl.when(jnp.logical_not(last))
    def _():
        gain_right.start()

    @pl.when(last)
    def _():
        gain_dp[mine] = gain_own[...]
        for turn in range(1, n_dp):
            across(turn, mine).start()
        for turn in range(1, n_dp):
            across(turn, lax.rem(mine + turn, n_dp)).wait_recv()
        total = gain_dp[0]
        for i in range(1, n_dp):
            total = total + gain_dp[i]
        gain_all[...] = total
        hand_gain_on()

    def relay_left(h, part):
        @pl.when(jnp.logical_not(last))
        def _():
            backward(h, part).wait_recv()

            @pl.when(jnp.logical_not(first))
            def _():
                bsend[h, piece(part)] = passed(bsend[h, piece(part)], brecv[h, piece(part)])
                backward(h, part).start()

    def local_grads(h):
        pre = pre_ref[:, cols(h)]
        grad_weights = (dot(pre, v_ref[:, cols(h)], 1, 1) * allow_ref[...]).astype(BF16)
        gq = dot(grad_weights, k_ref[:, cols(h)], 1, 0)
        gq = gq + dot(pre * head_ref[...], frecv[h].astype(BF16), 1, 1)
        gq_ref[:, cols(h)] = gq.astype(BF16)
        pk_ref[:, cols(h)] = dot(grad_weights, q_ref[:, cols(h)], 0, 0)

        pv_ref[:, cols(h)] = dot(wts_ref[h], pre, 0, 0)

    def finish(h):
        later = brecv[h].astype(BF16)
        gk = pk_ref[:, cols(h)] + dot(v_ref[:, cols(h)] * tail_ref[...], later, 1, 1)
        gk_ref[:, cols(h)] = gk.astype(BF16)
        gv = pv_ref[:, cols(h)] + dot(k_ref[:, cols(h)] * tail_ref[...], later, 1, 0)
        gv_ref[:, cols(h)] = gv.astype(BF16)

    ahead = jnp.where(first | last, heads, jnp.minimum(n_seq - 1 - place, heads))
    staggered(ahead, local_grads, relay_left, finish, hand_gain_on)

    @pl.when(first & (n_seq > 1))
    def _():
        hand_gain_on()

    @pl.when(last)
    def _():
        for turn in range(1, n_dp):
            across(turn, mine).wait_send()

    for turn in range(1, n_ten):
        exchange(turn, ten).wait_send()

    @pl.when(jnp.logical_not(last))
    def _():
        for h in range(heads):
            for part in range(CUTS):
                forward(h, part).wait_send()
        gain_right.wait_send()

    @pl.when(jnp.logical_not(first))
    def _():
        for h in range(heads):
            for part in range(CUTS):
                backward(h, part).wait_send()
        gain_left.wait_send()


def hand_out(*refs):
    count = len(refs) // 2
    copies = [
        pltpu.make_async_copy(refs[i], refs[count + i], refs[-1].at[i]) for i in range(count)
    ]
    for copy in copies:
        copy.start()
    for copy in copies:
        copy.wait()


def solution(mesh):
    sizes = (mesh.shape["dp"], mesh.shape["seq"], mesh.shape["tensor"])

    def shards(query, key_rows, value, gain, grad_out, start_offset):
        _, length, width = query.shape
        heads = width // DH
        hbm = pl.BlockSpec(memory_space=pltpu.HBM)
        vmem = pl.BlockSpec(memory_space=pltpu.VMEM)
        rows = jax.ShapeDtypeStruct((length, width), BF16)
        shapes = (rows,) * 4 + (jax.ShapeDtypeStruct((1, width), F32),)
        dma = pltpu.SemaphoreType.DMA
        flat = lambda a: a.reshape(length, width)
        outs = pl.pallas_call(
            functools.partial(kernel, sizes),
            out_shape=tuple(pltpu.VMEM(a.shape, a.dtype) for a in shapes),
            in_specs=[hbm] * 6,
            out_specs=(vmem,) * 5,
            scratch_shapes=[pltpu.SMEM(start_offset.shape, jnp.int32), pltpu.VMEM((1, width), F32)]
            + [pltpu.VMEM((length, width), BF16)] * 4
            + [
                pltpu.VMEM((length, length), F32),
                pltpu.VMEM((length, DH), BF16),
                pltpu.VMEM((length, DH), BF16),
                pltpu.VMEM((heads, length, length), BF16),
                pltpu.VMEM((length, width), F32),
                pltpu.VMEM((length, width), BF16),
                pltpu.VMEM((length, width), F32),
                pltpu.VMEM((length, width), F32),
                pltpu.VMEM((length, DH), F32),
                pltpu.VMEM((length, DH), F32),
            ]
            + [pltpu.VMEM((heads, DH, DH), F32)] * 4
            + [pltpu.VMEM((sizes[2], 2, length), F32), pltpu.VMEM((1, width), F32), pltpu.VMEM((1, width), F32)]
            + [pltpu.VMEM((sizes[0], 1, width), F32), pltpu.VMEM((1, width), F32)]
            + [dma((6,))] + [dma((heads, CUTS))] * 4
            + [dma((sizes[2],)), dma((sizes[2],)), dma((2,)), dma((2, sizes[0])), dma((2,))],
            compiler_params=pltpu.CompilerParams(
                collective_id=0, has_side_effects=True, vmem_limit_bytes=61 * 1024 * 1024
            ),
        )(start_offset, gain.reshape(1, width), flat(query), flat(key_rows), flat(value), flat(grad_out))
        *outs, grad_gain = pl.pallas_call(
            hand_out,
            out_shape=shapes,
            in_specs=[vmem] * 5,
            out_specs=(hbm,) * 5,
            scratch_shapes=[dma((5,))],
            compiler_params=pltpu.CompilerParams(vmem_limit_bytes=8 * 1024 * 1024),
        )(*outs)
        return tuple(a.reshape(1, length, width) for a in outs) + (grad_gain.reshape(width),)

    split = P("dp", "seq", "tensor")
    return jax.shard_map(
        shards,
        mesh=mesh,
        in_specs=(split, split, split, P("tensor"), split, P("dp", "seq")),
        out_specs=(split, split, split, split, P("tensor")),
        check_vma=False,
    )
```

```python
import functools

import jax
import jax.numpy as jnp
from jax import lax
from jax.experimental import pallas as pl
from jax.experimental.pallas import tpu as pltpu
from jax.sharding import PartitionSpec as P

DH = 128
BLK = 64
CH = 2048
EPS = 1e-05
CUTS = 4

SKIP = 1

MESH = pl.DeviceIdType.MESH
F32 = jnp.float32
BF16 = jnp.bfloat16


def dot(a, b, over_a, over_b):
    return lax.dot_general(a, b, (((over_a,), (over_b,)), ((), ())), preferred_element_type=F32)


def kernel(
    sizes, off_hbm, gain_hbm, q_hbm, k_hbm, v_hbm, g_hbm,
    out_ref, gq_ref, gk_ref, gv_ref, gg_ref,
    off_ref, gain_ref, q_ref, k_ref, v_ref, g_ref,
    allow_ref, head_ref, tail_ref, wts_ref, att_ref, pre_ref, pk_ref, pv_ref, sq_ref, raw_ref,
    fsend, frecv, bsend, brecv, stats, gain_own, gain_come, gain_dp, gain_all,
    ffar, bfar, flag, flag_left, flag_right,
    in_sem, fs_sem, fr_sem, bs_sem, br_sem, ss_sem, sr_sem, left_sem, dp_sem, right_sem,
    ffs_sem, ffr_sem, bfs_sem, bfr_sem, flag_sem,
):
    n_dp, n_seq, n_ten = sizes
    length, width = q_ref.shape
    heads = width // DH
    rows = DH // CUTS
    place = lax.axis_index("seq")
    ten = lax.axis_index("tensor")
    mine = lax.axis_index("dp")
    first, last = place == 0, place == n_seq - 1
    back = n_seq - 1 - place
    hub, back_hub = lax.rem(place, 2) == 1, lax.rem(back, 2) == 1
    far_out, far_in = hub & (back >= 2), hub & (place >= 3)
    back_far_out, back_far_in = back_hub & (place >= 2), back_hub & (back >= 3)
    near = heads - SKIP

    loads = [
        pltpu.make_async_copy(src, dst, in_sem.at[i])
        for i, (src, dst) in enumerate(
            (
                (off_hbm, off_ref), (k_hbm, k_ref), (v_hbm, v_ref),
                (q_hbm, q_ref), (g_hbm, g_ref), (gain_hbm, gain_ref),
            )
        )
    ]
    for load in loads:
        load.start()

    barrier = pltpu.get_barrier_semaphore()

    def greet(device):
        pl.semaphore_signal(barrier, inc=1, device_id=device, device_id_type=MESH)

    @pl.when(jnp.logical_not(last))
    def _():
        greet({"seq": place + 1})

    @pl.when(jnp.logical_not(first))
    def _():
        greet({"seq": place - 1})

    for turn in range(1, n_ten):
        greet({"tensor": lax.rem(ten + turn, n_ten)})
    for turn in range(1, n_dp):
        greet({"dp": lax.rem(mine + turn, n_dp)})

    @pl.when(far_in)
    def _():
        greet({"seq": place - 2})

    @pl.when(back_far_in)
    def _():
        greet({"seq": place + 2})

    greeted = n_ten - 1 + n_dp - 1 + jnp.where(last, 0, 1) + jnp.where(first, 0, 1)
    greeted = greeted + jnp.where(far_out, 1, 0) + jnp.where(back_far_out, 1, 0)

    def cols(h):
        return pl.ds(h * DH if isinstance(h, int) else pl.multiple_of(h * DH, DH), DH)

    def piece(part):
        return pl.ds(part * rows, rows)

    def forward(h, part):
        return pltpu.make_async_remote_copy(
            src_ref=fsend.at[h, piece(part)], dst_ref=frecv.at[h, piece(part)],
            send_sem=fs_sem.at[h, part], recv_sem=fr_sem.at[h, part],
            device_id={"seq": place + 1}, device_id_type=MESH,
        )

    def backward(h, part):
        return pltpu.make_async_remote_copy(
            src_ref=bsend.at[h, piece(part)], dst_ref=brecv.at[h, piece(part)],
            send_sem=bs_sem.at[h, part], recv_sem=br_sem.at[h, part],
            device_id={"seq": place - 1}, device_id_type=MESH,
        )

    def forward_far(h, part):
        return pltpu.make_async_remote_copy(
            src_ref=fsend.at[h, piece(part)], dst_ref=ffar.at[h - near, piece(part)],
            send_sem=ffs_sem.at[h - near, part], recv_sem=ffr_sem.at[h - near, part],
            device_id={"seq": place + 2}, device_id_type=MESH,
        )

    def backward_far(h, part):
        return pltpu.make_async_remote_copy(
            src_ref=bsend.at[h, piece(part)], dst_ref=bfar.at[h - near, piece(part)],
            send_sem=bfs_sem.at[h - near, part], recv_sem=bfr_sem.at[h - near, part],
            device_id={"seq": place - 2}, device_id_type=MESH,
        )

    flag_to_right = pltpu.make_async_remote_copy(
        src_ref=flag, dst_ref=flag_left, send_sem=flag_sem.at[0], recv_sem=flag_sem.at[1],
        device_id={"seq": place + 1}, device_id_type=MESH,
    )
    flag_to_left = pltpu.make_async_remote_copy(
        src_ref=flag, dst_ref=flag_right, send_sem=flag_sem.at[2], recv_sem=flag_sem.at[3],
        device_id={"seq": place - 1}, device_id_type=MESH,
    )

    def each_head(body, count=heads):
        def step(h, carry):
            body(h)
            return carry

        lax.fori_loop(0, count, step, 0)

    def each_head_apart(body):
        each_head(body, near)
        for h in range(near, heads):
            body(h)

    loads[0].wait()
    starts_at = []
    starts = jnp.int32(0)
    for j in range(off_ref.shape[1]):
        offset = off_ref[0, j]
        starts_at.append(jnp.where(offset < BLK, j * BLK + offset, length))
        starts = starts + jnp.where(offset < BLK, 1, 0)

    def labels(positions):
        total = jnp.zeros(positions.shape, jnp.int32)
        for at in starts_at:
            total = total + jnp.where(positions >= at, 1, 0)
        return total

    label = labels(lax.broadcasted_iota(jnp.int32, (length, DH), 0))
    head_ref[...] = jnp.where(label == 0, 1.0, 0.0).astype(BF16)
    tail_ref[...] = jnp.where(label == starts, 1.0, 0.0).astype(BF16)

    def passed(own, come):
        keep = jnp.full(come.shape, starts, jnp.int32) == 0
        return own + jnp.where(keep, come, 0.0)

    loads[1].wait()
    loads[2].wait()

    def tail(h):
        fsend[h] = dot(k_ref[:, cols(h)] * tail_ref[...], v_ref[:, cols(h)], 0, 0)

    def launch(h):
        @pl.when(first & (n_seq > 1))
        def _():
            for part in range(CUTS):
                forward(h, part).start()

    tail(0)
    pl.semaphore_wait(barrier, greeted)
    launch(0)
    flag[...] = jnp.where(jnp.full(flag.shape, starts, jnp.int32) == 0, 1.0, 0.0)

    @pl.when(jnp.logical_not(last))
    def _():
        flag_to_right.start()

    @pl.when(jnp.logical_not(first))
    def _():
        flag_to_left.start()

    def tails(h, carry):
        tail(h)
        launch(h)
        return carry

    lax.fori_loop(1, heads, tails, 0)

    @pl.when(jnp.logical_not(first | last | hub))
    def _():
        for h in range(near, heads):
            for part in range(CUTS):
                forward(h, part).start()

    def joined(own, come, flags):
        return own + jnp.where(jnp.broadcast_to(flags[0:1, :], come.shape) > 0, come, 0.0)

    rows_at = lax.broadcasted_iota(jnp.int32, (length, length), 0)
    cols_at = lax.broadcasted_iota(jnp.int32, (length, length), 1)
    allow_ref[...] = jnp.where(
        (labels(rows_at) == labels(cols_at)) & (cols_at <= rows_at), 1.0, 0.0
    )

    @pl.when(first)
    def _():
        frecv[...] = jnp.zeros_like(frecv)

    @pl.when(last)
    def _():
        brecv[...] = jnp.zeros_like(brecv)

    sq_ref[...] = jnp.zeros_like(sq_ref)
    raw_ref[...] = jnp.zeros_like(raw_ref)
    for load in loads[3:]:
        load.wait()

    def relay_right(h, part):
        if isinstance(h, int):
            far_right(h, part)
            return

        @pl.when(jnp.logical_not(first))
        def _():
            forward(h, part).wait_recv()

            @pl.when(jnp.logical_not(last))
            def _():
                fsend[h, piece(part)] = passed(fsend[h, piece(part)], frecv[h, piece(part)])
                forward(h, part).start()

    def far_right(h, part):
        at = piece(part)

        @pl.when(jnp.logical_not(first))
        def _():
            if h == near and part == 0:
                flag_to_right.wait_recv()
            forward(h, part).wait_recv()

        @pl.when(far_in)
        def _():
            forward_far(h, part).wait_recv()
            frecv[h, at] = joined(frecv[h, at], ffar[h - near, at], flag_left)

        @pl.when(hub & jnp.logical_not(last))
        def _():
            fsend[h, at] = passed(fsend[h, at], frecv[h, at])

        @pl.when(far_out)
        def _():
            forward_far(h, part).start()

        if part == CUTS - 1:
            @pl.when(hub & jnp.logical_not(last))
            def _():
                for piece_at in range(CUTS):
                    forward(h, piece_at).start()

    def attend(h):
        scores = dot(q_ref[:, cols(h)], k_ref[:, cols(h)], 1, 1)
        wts_ref[h] = (scores * allow_ref[...]).astype(BF16)
        att_ref[:, cols(h)] = dot(wts_ref[h], v_ref[:, cols(h)], 1, 0)

    def add_carried(h):
        attended = att_ref[:, cols(h)] + dot(
            q_ref[:, cols(h)] * head_ref[...], frecv[h].astype(BF16), 1, 0
        )
        att_ref[:, cols(h)] = attended
        sq_ref[...] = sq_ref[...] + attended * attended
        raw_ref[...] = raw_ref[...] + gain_ref[:, cols(h)] * g_ref[:, cols(h)].astype(F32) * attended

    def staggered(ahead, local, relay, finish, passed_on):
        def before(h, carry):
            local(h)
            return carry

        lax.fori_loop(0, ahead, before, 0)

        @pl.when(first | last)
        def _():
            def step(h):
                for part in range(CUTS):
                    relay(h, part)
                finish(h)

            each_head_apart(step)

        @pl.when(jnp.logical_not(first | last))
        def _():
            def step(h):
                for part in range(CUTS):
                    relay(h, part)

            each_head_apart(step)
            passed_on()

            def rest(h):
                @pl.when(h >= ahead)
                def _():
                    local(h)

                finish(h)

            each_head(rest)

    ahead = jnp.where(first | last, heads, jnp.minimum(2 * place - 1, heads))
    staggered(ahead, attend, relay_right, add_carried, lambda: None)

    stats[ten, 0:1, :] = jnp.sum(sq_ref[...].T, axis=0, keepdims=True)
    stats[ten, 1:2, :] = jnp.sum(raw_ref[...].T, axis=0, keepdims=True)

    def exchange(turn, slot):
        return pltpu.make_async_remote_copy(
            src_ref=stats.at[slot], dst_ref=stats.at[slot],
            send_sem=ss_sem.at[turn], recv_sem=sr_sem.at[slot],
            device_id={"tensor": lax.rem(ten + turn, n_ten)}, device_id_type=MESH,
        )

    for turn in range(1, n_ten):
        exchange(turn, ten).start()
    for turn in range(1, n_ten):
        exchange(turn, lax.rem(ten + turn, n_ten)).wait_recv()
    totals = stats[0]
    for t in range(1, n_ten):
        totals = totals + stats[t]
    inverse = lax.rsqrt(totals[0:1, :] / CH + EPS)
    slope = inverse * inverse * (totals[1:2, :] / CH)
    sq_ref[...] = jnp.broadcast_to(inverse, (DH, length)).T
    raw_ref[...] = jnp.broadcast_to(slope, (DH, length)).T

    def before_norm(h):
        upstream = g_ref[:, cols(h)].astype(F32)
        pre = sq_ref[...] * (gain_ref[:, cols(h)] * upstream - att_ref[:, cols(h)] * raw_ref[...])
        pre = pre.astype(BF16)
        pre_ref[:, cols(h)] = pre
        bsend[h] = dot(q_ref[:, cols(h)] * head_ref[...], pre, 0, 0)

        @pl.when(last & (n_seq > 1))
        def _():
            for part in range(CUTS):
                backward(h, part).start()

    each_head(before_norm)

    @pl.when(jnp.logical_not(first | last | back_hub))
    def _():
        for h in range(near, heads):
            for part in range(CUTS):
                backward(h, part).start()

    def after_norm(h):
        normed = att_ref[:, cols(h)] * sq_ref[...]
        out_ref[:, cols(h)] = (gain_ref[:, cols(h)] * normed).astype(BF16)
        gain_own[:, cols(h)] = jnp.sum(
            g_ref[:, cols(h)].astype(F32) * normed, axis=0, keepdims=True
        )

    for h in range(heads):
        after_norm(h)

    gain_right = pltpu.make_async_remote_copy(
        src_ref=gain_own, dst_ref=gain_come, send_sem=right_sem.at[0], recv_sem=right_sem.at[1],
        device_id={"seq": place + 1}, device_id_type=MESH,
    )
    gain_left = pltpu.make_async_remote_copy(
        src_ref=gain_all, dst_ref=gain_all, send_sem=left_sem.at[0], recv_sem=left_sem.at[1],
        device_id={"seq": place - 1}, device_id_type=MESH,
    )

    def across(turn, slot):
        return pltpu.make_async_remote_copy(
            src_ref=gain_dp.at[slot], dst_ref=gain_dp.at[slot],
            send_sem=dp_sem.at[0, turn], recv_sem=dp_sem.at[1, slot],
            device_id={"dp": lax.rem(mine + turn, n_dp)}, device_id_type=MESH,
        )

    def hand_gain_on():
        @pl.when(jnp.logical_not(last))
        def _():
            gain_left.wait_recv()

        @pl.when(jnp.logical_not(first))
        def _():
            gain_left.start()

        gg_ref[...] = gain_all[...]

    @pl.when(jnp.logical_not(first))
    def _():
        gain_right.wait_recv()
        gain_own[...] = gain_own[...] + gain_come[...]

    @pl.when(jnp.logical_not(last))
    def _():
        gain_right.start()

    @pl.when(last)
    def _():
        gain_dp[mine] = gain_own[...]
        for turn in range(1, n_dp):
            across(turn, mine).start()
        for turn in range(1, n_dp):
            across(turn, lax.rem(mine + turn, n_dp)).wait_recv()
        total = gain_dp[0]
        for i in range(1, n_dp):
            total = total + gain_dp[i]
        gain_all[...] = total
        hand_gain_on()

    def relay_left(h, part):
        if isinstance(h, int):
            far_left(h, part)
            return

        @pl.when(jnp.logical_not(last))
        def _():
            backward(h, part).wait_recv()

            @pl.when(jnp.logical_not(first))
            def _():
                bsend[h, piece(part)] = passed(bsend[h, piece(part)], brecv[h, piece(part)])
                backward(h, part).start()

    def far_left(h, part):
        at = piece(part)

        @pl.when(jnp.logical_not(last))
        def _():
            if h == near and part == 0:
                flag_to_left.wait_recv()
            backward(h, part).wait_recv()

        @pl.when(back_far_in)
        def _():
            backward_far(h, part).wait_recv()
            brecv[h, at] = joined(brecv[h, at], bfar[h - near, at], flag_right)

        @pl.when(back_hub & jnp.logical_not(first))
        def _():
            bsend[h, at] = passed(bsend[h, at], brecv[h, at])

        @pl.when(back_far_out)
        def _():
            backward_far(h, part).start()

        if part == CUTS - 1:
            @pl.when(back_hub & jnp.logical_not(first))
            def _():
                for piece_at in range(CUTS):
                    backward(h, piece_at).start()

    def local_grads(h):
        pre = pre_ref[:, cols(h)]
        grad_weights = (dot(pre, v_ref[:, cols(h)], 1, 1) * allow_ref[...]).astype(BF16)
        gq = dot(grad_weights, k_ref[:, cols(h)], 1, 0)
        gq = gq + dot(pre * head_ref[...], frecv[h].astype(BF16), 1, 1)
        gq_ref[:, cols(h)] = gq.astype(BF16)
        pk_ref[:, cols(h)] = dot(grad_weights, q_ref[:, cols(h)], 0, 0)

        pv_ref[:, cols(h)] = dot(wts_ref[h], pre, 0, 0)

    def finish(h):
        later = brecv[h].astype(BF16)
        gk = pk_ref[:, cols(h)] + dot(v_ref[:, cols(h)] * tail_ref[...], later, 1, 1)
        gk_ref[:, cols(h)] = gk.astype(BF16)
        gv = pv_ref[:, cols(h)] + dot(k_ref[:, cols(h)] * tail_ref[...], later, 1, 0)
        gv_ref[:, cols(h)] = gv.astype(BF16)

    ahead = jnp.where(first | last, heads, jnp.minimum(n_seq - 1 - place, heads))
    staggered(ahead, local_grads, relay_left, finish, hand_gain_on)

    @pl.when(first & (n_seq > 1))
    def _():
        hand_gain_on()

    @pl.when(last)
    def _():
        for turn in range(1, n_dp):
            across(turn, mine).wait_send()

    for turn in range(1, n_ten):
        exchange(turn, ten).wait_send()

    @pl.when(jnp.logical_not(last))
    def _():
        for h in range(heads):
            for part in range(CUTS):
                forward(h, part).wait_send()
        gain_right.wait_send()
        flag_to_right.wait_send()

    @pl.when(far_out)
    def _():
        for h in range(near, heads):
            for part in range(CUTS):
                forward_far(h, part).wait_send()

    @pl.when(back_far_out)
    def _():
        for h in range(near, heads):
            for part in range(CUTS):
                backward_far(h, part).wait_send()

    @pl.when(jnp.logical_not(first))
    def _():
        for h in range(heads):
            for part in range(CUTS):
                backward(h, part).wait_send()
        gain_left.wait_send()
        flag_to_left.wait_send()


def hand_out(*refs):
    count = len(refs) // 2
    copies = [
        pltpu.make_async_copy(refs[i], refs[count + i], refs[-1].at[i]) for i in range(count)
    ]
    for copy in copies:
        copy.start()
    for copy in copies:
        copy.wait()


def solution(mesh):
    sizes = (mesh.shape["dp"], mesh.shape["seq"], mesh.shape["tensor"])

    def shards(query, key_rows, value, gain, grad_out, start_offset):
        _, length, width = query.shape
        heads = width // DH
        hbm = pl.BlockSpec(memory_space=pltpu.HBM)
        vmem = pl.BlockSpec(memory_space=pltpu.VMEM)
        rows = jax.ShapeDtypeStruct((length, width), BF16)
        shapes = (rows,) * 4 + (jax.ShapeDtypeStruct((1, width), F32),)
        dma = pltpu.SemaphoreType.DMA
        flat = lambda a: a.reshape(length, width)
        outs = pl.pallas_call(
            functools.partial(kernel, sizes),
            out_shape=tuple(pltpu.VMEM(a.shape, a.dtype) for a in shapes),
            in_specs=[hbm] * 6,
            out_specs=(vmem,) * 5,
            scratch_shapes=[pltpu.SMEM(start_offset.shape, jnp.int32), pltpu.VMEM((1, width), F32)]
            + [pltpu.VMEM((length, width), BF16)] * 4
            + [
                pltpu.VMEM((length, length), F32),
                pltpu.VMEM((length, DH), BF16),
                pltpu.VMEM((length, DH), BF16),
                pltpu.VMEM((heads, length, length), BF16),
                pltpu.VMEM((length, width), F32),
                pltpu.VMEM((length, width), BF16),
                pltpu.VMEM((length, width), F32),
                pltpu.VMEM((length, width), F32),
                pltpu.VMEM((length, DH), F32),
                pltpu.VMEM((length, DH), F32),
            ]
            + [pltpu.VMEM((heads, DH, DH), F32)] * 4
            + [pltpu.VMEM((sizes[2], 2, length), F32), pltpu.VMEM((1, width), F32), pltpu.VMEM((1, width), F32)]
            + [pltpu.VMEM((sizes[0], 1, width), F32), pltpu.VMEM((1, width), F32)]
            + [pltpu.VMEM((SKIP, DH, DH), F32)] * 2
            + [pltpu.VMEM((8, DH), F32)] * 3
            + [dma((6,))] + [dma((heads, CUTS))] * 4
            + [dma((sizes[2],)), dma((sizes[2],)), dma((2,)), dma((2, sizes[0])), dma((2,))]
            + [dma((SKIP, CUTS))] * 4
            + [dma((4,))],
            compiler_params=pltpu.CompilerParams(
                collective_id=0, has_side_effects=True, vmem_limit_bytes=61 * 1024 * 1024
            ),
        )(start_offset, gain.reshape(1, width), flat(query), flat(key_rows), flat(value), flat(grad_out))
        *outs, grad_gain = pl.pallas_call(
            hand_out,
            out_shape=shapes,
            in_specs=[vmem] * 5,
            out_specs=(hbm,) * 5,
            scratch_shapes=[dma((5,))],
            compiler_params=pltpu.CompilerParams(vmem_limit_bytes=8 * 1024 * 1024),
        )(*outs)
        return tuple(a.reshape(1, length, width) for a in outs) + (grad_gain.reshape(width),)

    split = P("dp", "seq", "tensor")
    return jax.shard_map(
        shards,
        mesh=mesh,
        in_specs=(split, split, split, P("tensor"), split, P("dp", "seq")),
        out_specs=(split, split, split, split, P("tensor")),
        check_vma=False,
    )
```

```python
import functools

import jax
import jax.numpy as jnp
from jax import lax
from jax.experimental import pallas as pl
from jax.experimental.pallas import tpu as pltpu
from jax.sharding import PartitionSpec as P

DH = 128
BLK = 64
CH = 2048
EPS = 1e-05
CUTS = 4

MESH = pl.DeviceIdType.MESH
F32 = jnp.float32
BF16 = jnp.bfloat16


def dot(a, b, over_a, over_b):
    return lax.dot_general(a, b, (((over_a,), (over_b,)), ((), ())), preferred_element_type=F32)


def kernel(
    sizes, off_hbm, gain_hbm, q_hbm, k_hbm, v_hbm, g_hbm,
    out_ref, gq_ref, gk_ref, gv_ref, gg_ref,
    off_ref, gain_ref, q_ref, k_ref, v_ref, g_ref,
    allow_ref, head_ref, tail_ref, wts_ref, att_ref, pre_ref, pk_ref, pv_ref, sq_ref, raw_ref,
    fsend, frecv, bsend, brecv, stats, gain_own, gain_come, gain_dp, gain_all,
    in_sem, fs_sem, fr_sem, bs_sem, br_sem, ss_sem, sr_sem, left_sem, dp_sem, right_sem, turn_sem,
):
    n_dp, n_seq, n_ten = sizes
    length, width = q_ref.shape
    heads = width // DH
    rows = DH // CUTS
    place = lax.axis_index("seq")
    ten = lax.axis_index("tensor")
    mine = lax.axis_index("dp")
    first, last = place == 0, place == n_seq - 1

    loads = [
        pltpu.make_async_copy(src, dst, in_sem.at[i])
        for i, (src, dst) in enumerate(
            (
                (off_hbm, off_ref), (k_hbm, k_ref), (v_hbm, v_ref),
                (q_hbm, q_ref), (g_hbm, g_ref), (gain_hbm, gain_ref),
            )
        )
    ]
    for load in loads:
        load.start()

    barrier = pltpu.get_barrier_semaphore()

    def greet(device):
        pl.semaphore_signal(barrier, inc=1, device_id=device, device_id_type=MESH)

    @pl.when(jnp.logical_not(last))
    def _():
        greet({"seq": place + 1})

    @pl.when(jnp.logical_not(first))
    def _():
        greet({"seq": place - 1})

    for turn in range(1, n_ten):
        greet({"tensor": lax.rem(ten + turn, n_ten)})
    for turn in range(1, n_dp):
        greet({"dp": lax.rem(mine + turn, n_dp)})
    greeted = n_ten - 1 + n_dp - 1 + jnp.where(last, 0, 1) + jnp.where(first, 0, 1)

    def cols(h):
        return pl.ds(h * DH if isinstance(h, int) else pl.multiple_of(h * DH, DH), DH)

    def piece(part):
        return pl.ds(part * rows, rows)

    def forward(h, part):
        return pltpu.make_async_remote_copy(
            src_ref=fsend.at[h, piece(part)], dst_ref=frecv.at[h, piece(part)],
            send_sem=fs_sem.at[h, part], recv_sem=fr_sem.at[h, part],
            device_id={"seq": place + 1}, device_id_type=MESH,
        )

    def backward(h, part):
        return pltpu.make_async_remote_copy(
            src_ref=bsend.at[h, piece(part)], dst_ref=brecv.at[h, piece(part)],
            send_sem=bs_sem.at[h, part], recv_sem=br_sem.at[h, part],
            device_id={"seq": place - 1}, device_id_type=MESH,
        )

    def each_head(body):
        def step(h, carry):
            body(h)
            return carry

        lax.fori_loop(0, heads, step, 0)

    loads[0].wait()
    starts_at = []
    starts = jnp.int32(0)
    for j in range(off_ref.shape[1]):
        offset = off_ref[0, j]
        starts_at.append(jnp.where(offset < BLK, j * BLK + offset, length))
        starts = starts + jnp.where(offset < BLK, 1, 0)

    def labels(positions):
        total = jnp.zeros(positions.shape, jnp.int32)
        for at in starts_at:
            total = total + jnp.where(positions >= at, 1, 0)
        return total

    label = labels(lax.broadcasted_iota(jnp.int32, (length, DH), 0))
    head_ref[...] = jnp.where(label == 0, 1.0, 0.0).astype(BF16)
    tail_ref[...] = jnp.where(label == starts, 1.0, 0.0).astype(BF16)

    def passed(own, come):
        keep = jnp.full(come.shape, starts, jnp.int32) == 0
        return own + jnp.where(keep, come, 0.0)

    loads[1].wait()
    loads[2].wait()

    def tail(h):
        fsend[h] = dot(k_ref[:, cols(h)] * tail_ref[...], v_ref[:, cols(h)], 0, 0)

    leads = first & (mine < n_dp - 1) & (n_seq > 1)
    follows = first & (mine > 0) & (n_seq > 1)

    def launch(h):
        @pl.when(first & (mine == 0) & (n_seq > 1))
        def _():
            for part in range(CUTS):
                forward(h, part).start()

    tail(0)
    pl.semaphore_wait(barrier, greeted)
    launch(0)

    def tails(h, carry):
        tail(h)
        launch(h)
        return carry

    lax.fori_loop(1, heads, tails, 0)

    @pl.when(follows)
    def _():
        pl.semaphore_wait(turn_sem, 1)
        for h in range(heads):
            for part in range(CUTS):
                forward(h, part).start()

    @pl.when(leads)
    def _():
        for h in range(heads - 1):
            for part in range(CUTS):
                forward(h, part).wait_send()
        pl.semaphore_signal(turn_sem, inc=1, device_id={"dp": mine + 1}, device_id_type=MESH)

    rows_at = lax.broadcasted_iota(jnp.int32, (length, length), 0)
    cols_at = lax.broadcasted_iota(jnp.int32, (length, length), 1)
    allow_ref[...] = jnp.where(
        (labels(rows_at) == labels(cols_at)) & (cols_at <= rows_at), 1.0, 0.0
    )

    @pl.when(first)
    def _():
        frecv[...] = jnp.zeros_like(frecv)

    @pl.when(last)
    def _():
        brecv[...] = jnp.zeros_like(brecv)

    sq_ref[...] = jnp.zeros_like(sq_ref)
    raw_ref[...] = jnp.zeros_like(raw_ref)
    for load in loads[3:]:
        load.wait()

    def relay_right(h, part):
        @pl.when(jnp.logical_not(first))
        def _():
            forward(h, part).wait_recv()

            @pl.when(jnp.logical_not(last))
            def _():
                fsend[h, piece(part)] = passed(fsend[h, piece(part)], frecv[h, piece(part)])
                forward(h, part).start()

    def attend(h):
        scores = dot(q_ref[:, cols(h)], k_ref[:, cols(h)], 1, 1)
        wts_ref[h] = (scores * allow_ref[...]).astype(BF16)
        att_ref[:, cols(h)] = dot(wts_ref[h], v_ref[:, cols(h)], 1, 0)

    def add_carried(h):
        attended = att_ref[:, cols(h)] + dot(
            q_ref[:, cols(h)] * head_ref[...], frecv[h].astype(BF16), 1, 0
        )
        att_ref[:, cols(h)] = attended
        sq_ref[...] = sq_ref[...] + attended * attended
        raw_ref[...] = raw_ref[...] + gain_ref[:, cols(h)] * g_ref[:, cols(h)].astype(F32) * attended

    def staggered(ahead, local, relay, finish, passed_on):
        def before(h, carry):
            local(h)
            return carry

        lax.fori_loop(0, ahead, before, 0)

        @pl.when(first | last)
        def _():
            def step(h):
                for part in range(CUTS):
                    relay(h, part)
                finish(h)

            each_head(step)

        @pl.when(jnp.logical_not(first | last))
        def _():
            def step(h):
                for part in range(CUTS):
                    relay(h, part)

            each_head(step)
            passed_on()

            def rest(h):
                @pl.when(h >= ahead)
                def _():
                    local(h)

                finish(h)

            each_head(rest)

    ahead = jnp.where(first | last, heads, jnp.minimum(2 * place - 1, heads))
    staggered(ahead, attend, relay_right, add_carried, lambda: None)

    stats[ten, 0:1, :] = jnp.sum(sq_ref[...].T, axis=0, keepdims=True)
    stats[ten, 1:2, :] = jnp.sum(raw_ref[...].T, axis=0, keepdims=True)

    def exchange(turn, slot):
        return pltpu.make_async_remote_copy(
            src_ref=stats.at[slot], dst_ref=stats.at[slot],
            send_sem=ss_sem.at[turn], recv_sem=sr_sem.at[slot],
            device_id={"tensor": lax.rem(ten + turn, n_ten)}, device_id_type=MESH,
        )

    for turn in range(1, n_ten):
        exchange(turn, ten).start()
    for turn in range(1, n_ten):
        exchange(turn, lax.rem(ten + turn, n_ten)).wait_recv()
    totals = stats[0]
    for t in range(1, n_ten):
        totals = totals + stats[t]
    inverse = lax.rsqrt(totals[0:1, :] / CH + EPS)
    slope = inverse * inverse * (totals[1:2, :] / CH)
    sq_ref[...] = jnp.broadcast_to(inverse, (DH, length)).T
    raw_ref[...] = jnp.broadcast_to(slope, (DH, length)).T

    def before_norm(h):
        upstream = g_ref[:, cols(h)].astype(F32)
        pre = sq_ref[...] * (gain_ref[:, cols(h)] * upstream - att_ref[:, cols(h)] * raw_ref[...])
        pre = pre.astype(BF16)
        pre_ref[:, cols(h)] = pre
        bsend[h] = dot(q_ref[:, cols(h)] * head_ref[...], pre, 0, 0)

        @pl.when(last & (n_seq > 1))
        def _():
            for part in range(CUTS):
                backward(h, part).start()

    each_head(before_norm)

    def after_norm(h):
        normed = att_ref[:, cols(h)] * sq_ref[...]
        out_ref[:, cols(h)] = (gain_ref[:, cols(h)] * normed).astype(BF16)
        gain_own[:, cols(h)] = jnp.sum(
            g_ref[:, cols(h)].astype(F32) * normed, axis=0, keepdims=True
        )

    for h in range(heads):
        after_norm(h)

    gain_right = pltpu.make_async_remote_copy(
        src_ref=gain_own, dst_ref=gain_come, send_sem=right_sem.at[0], recv_sem=right_sem.at[1],
        device_id={"seq": place + 1}, device_id_type=MESH,
    )
    gain_left = pltpu.make_async_remote_copy(
        src_ref=gain_all, dst_ref=gain_all, send_sem=left_sem.at[0], recv_sem=left_sem.at[1],
        device_id={"seq": place - 1}, device_id_type=MESH,
    )

    def across(turn, slot):
        return pltpu.make_async_remote_copy(
            src_ref=gain_dp.at[slot], dst_ref=gain_dp.at[slot],
            send_sem=dp_sem.at[0, turn], recv_sem=dp_sem.at[1, slot],
            device_id={"dp": lax.rem(mine + turn, n_dp)}, device_id_type=MESH,
        )

    def hand_gain_on():
        @pl.when(jnp.logical_not(last))
        def _():
            gain_left.wait_recv()

        @pl.when(jnp.logical_not(first))
        def _():
            gain_left.start()

        gg_ref[...] = gain_all[...]

    @pl.when(jnp.logical_not(first))
    def _():
        gain_right.wait_recv()
        gain_own[...] = gain_own[...] + gain_come[...]

    @pl.when(jnp.logical_not(last))
    def _():
        gain_right.start()

    @pl.when(last)
    def _():
        gain_dp[mine] = gain_own[...]
        for turn in range(1, n_dp):
            across(turn, mine).start()
        for turn in range(1, n_dp):
            across(turn, lax.rem(mine + turn, n_dp)).wait_recv()
        total = gain_dp[0]
        for i in range(1, n_dp):
            total = total + gain_dp[i]
        gain_all[...] = total
        hand_gain_on()

    def relay_left(h, part):
        @pl.when(jnp.logical_not(last))
        def _():
            backward(h, part).wait_recv()

            @pl.when(jnp.logical_not(first))
            def _():
                bsend[h, piece(part)] = passed(bsend[h, piece(part)], brecv[h, piece(part)])
                backward(h, part).start()

    def local_grads(h):
        pre = pre_ref[:, cols(h)]
        grad_weights = (dot(pre, v_ref[:, cols(h)], 1, 1) * allow_ref[...]).astype(BF16)
        gq = dot(grad_weights, k_ref[:, cols(h)], 1, 0)
        gq = gq + dot(pre * head_ref[...], frecv[h].astype(BF16), 1, 1)
        gq_ref[:, cols(h)] = gq.astype(BF16)
        pk_ref[:, cols(h)] = dot(grad_weights, q_ref[:, cols(h)], 0, 0)

        pv_ref[:, cols(h)] = dot(wts_ref[h], pre, 0, 0)

    def finish(h):
        later = brecv[h].astype(BF16)
        gk = pk_ref[:, cols(h)] + dot(v_ref[:, cols(h)] * tail_ref[...], later, 1, 1)
        gk_ref[:, cols(h)] = gk.astype(BF16)
        gv = pv_ref[:, cols(h)] + dot(k_ref[:, cols(h)] * tail_ref[...], later, 1, 0)
        gv_ref[:, cols(h)] = gv.astype(BF16)

    ahead = jnp.where(first | last, heads, jnp.minimum(n_seq - 1 - place, heads))
    staggered(ahead, local_grads, relay_left, finish, hand_gain_on)

    @pl.when(first & (n_seq > 1))
    def _():
        hand_gain_on()

    @pl.when(last)
    def _():
        for turn in range(1, n_dp):
            across(turn, mine).wait_send()

    for turn in range(1, n_ten):
        exchange(turn, ten).wait_send()

    @pl.when(jnp.logical_not(last))
    def _():
        @pl.when(jnp.logical_not(leads))
        def _():
            for h in range(heads - 1):
                for part in range(CUTS):
                    forward(h, part).wait_send()

        for part in range(CUTS):
            forward(heads - 1, part).wait_send()
        gain_right.wait_send()

    @pl.when(jnp.logical_not(first))
    def _():
        for h in range(heads):
            for part in range(CUTS):
                backward(h, part).wait_send()
        gain_left.wait_send()


def hand_out(*refs):
    count = len(refs) // 2
    copies = [
        pltpu.make_async_copy(refs[i], refs[count + i], refs[-1].at[i]) for i in range(count)
    ]
    for copy in copies:
        copy.start()
    for copy in copies:
        copy.wait()


def solution(mesh):
    sizes = (mesh.shape["dp"], mesh.shape["seq"], mesh.shape["tensor"])

    def shards(query, key_rows, value, gain, grad_out, start_offset):
        _, length, width = query.shape
        heads = width // DH
        hbm = pl.BlockSpec(memory_space=pltpu.HBM)
        vmem = pl.BlockSpec(memory_space=pltpu.VMEM)
        rows = jax.ShapeDtypeStruct((length, width), BF16)
        shapes = (rows,) * 4 + (jax.ShapeDtypeStruct((1, width), F32),)
        dma = pltpu.SemaphoreType.DMA
        flat = lambda a: a.reshape(length, width)
        outs = pl.pallas_call(
            functools.partial(kernel, sizes),
            out_shape=tuple(pltpu.VMEM(a.shape, a.dtype) for a in shapes),
            in_specs=[hbm] * 6,
            out_specs=(vmem,) * 5,
            scratch_shapes=[pltpu.SMEM(start_offset.shape, jnp.int32), pltpu.VMEM((1, width), F32)]
            + [pltpu.VMEM((length, width), BF16)] * 4
            + [
                pltpu.VMEM((length, length), F32),
                pltpu.VMEM((length, DH), BF16),
                pltpu.VMEM((length, DH), BF16),
                pltpu.VMEM((heads, length, length), BF16),
                pltpu.VMEM((length, width), F32),
                pltpu.VMEM((length, width), BF16),
                pltpu.VMEM((length, width), F32),
                pltpu.VMEM((length, width), F32),
                pltpu.VMEM((length, DH), F32),
                pltpu.VMEM((length, DH), F32),
            ]
            + [pltpu.VMEM((heads, DH, DH), F32)] * 4
            + [pltpu.VMEM((sizes[2], 2, length), F32), pltpu.VMEM((1, width), F32), pltpu.VMEM((1, width), F32)]
            + [pltpu.VMEM((sizes[0], 1, width), F32), pltpu.VMEM((1, width), F32)]
            + [dma((6,))] + [dma((heads, CUTS))] * 4
            + [dma((sizes[2],)), dma((sizes[2],)), dma((2,)), dma((2, sizes[0])), dma((2,))]
            + [pltpu.SemaphoreType.REGULAR],
            compiler_params=pltpu.CompilerParams(
                collective_id=0, has_side_effects=True, vmem_limit_bytes=61 * 1024 * 1024
            ),
        )(start_offset, gain.reshape(1, width), flat(query), flat(key_rows), flat(value), flat(grad_out))
        *outs, grad_gain = pl.pallas_call(
            hand_out,
            out_shape=shapes,
            in_specs=[vmem] * 5,
            out_specs=(hbm,) * 5,
            scratch_shapes=[dma((5,))],
            compiler_params=pltpu.CompilerParams(vmem_limit_bytes=8 * 1024 * 1024),
        )(*outs)
        return tuple(a.reshape(1, length, width) for a in outs) + (grad_gain.reshape(width),)

    split = P("dp", "seq", "tensor")
    return jax.shard_map(
        shards,
        mesh=mesh,
        in_specs=(split, split, split, P("tensor"), split, P("dp", "seq")),
        out_specs=(split, split, split, split, P("tensor")),
        check_vma=False,
    )
```

```python
import functools

import jax
import jax.numpy as jnp
from jax import lax
from jax.experimental import pallas as pl
from jax.experimental.pallas import tpu as pltpu
from jax.sharding import PartitionSpec as P

DH = 128
BLK = 64
CH = 2048
EPS = 1e-05
CUTS = 4

MESH = pl.DeviceIdType.MESH
F32 = jnp.float32
BF16 = jnp.bfloat16


def dot(a, b, over_a, over_b):
    return lax.dot_general(a, b, (((over_a,), (over_b,)), ((), ())), preferred_element_type=F32)


def kernel(
    sizes, off_hbm, gain_hbm, q_hbm, k_hbm, v_hbm, g_hbm,
    out_ref, gq_ref, gk_ref, gv_ref, gg_ref,
    off_ref, gain_ref, q_ref, k_ref, v_ref, g_ref,
    allow_ref, head_ref, tail_ref, wts_ref, att_ref, pre_ref, pk_ref, pv_ref, sq_ref, raw_ref,
    fsend, frecv, bsend, brecv, stats, gain_own, gain_come, gain_dp,
    in_sem, fs_sem, fr_sem, bs_sem, br_sem, ss_sem, sr_sem, left_sem, dp_sem, right_sem,
):
    n_dp, n_seq, n_ten = sizes
    length, width = q_ref.shape
    heads = width // DH
    rows = DH // CUTS
    place = lax.axis_index("seq")
    ten = lax.axis_index("tensor")
    mine = lax.axis_index("dp")
    first, last = place == 0, place == n_seq - 1
    back = n_seq - 1 - place
    group = n_dp * n_seq

    loads = [
        pltpu.make_async_copy(src, dst, in_sem.at[i])
        for i, (src, dst) in enumerate(
            (
                (off_hbm, off_ref), (k_hbm, k_ref), (v_hbm, v_ref),
                (q_hbm, q_ref), (g_hbm, g_ref), (gain_hbm, gain_ref),
            )
        )
    ]
    for load in loads:
        load.start()

    barrier = pltpu.get_barrier_semaphore()

    def greet(device):
        pl.semaphore_signal(barrier, inc=1, device_id=device, device_id_type=MESH)

    @pl.when(jnp.logical_not(last))
    def _():
        greet({"seq": place + 1})

    @pl.when(jnp.logical_not(first))
    def _():
        greet({"seq": place - 1})

    for turn in range(1, n_ten):
        greet({"tensor": lax.rem(ten + turn, n_ten)})
    for turn in range(1, n_dp):
        greet({"dp": lax.rem(mine + turn, n_dp)})

    for d in range(n_dp):
        @pl.when((back > 1) | ((back == 1) & (mine != d)))
        def _():
            greet({"dp": d, "seq": n_seq - 1})

    greeted = n_ten - 1 + n_dp - 1 + jnp.where(last, 0, 1) + jnp.where(first, 0, 1)
    greeted = greeted + jnp.where(last, n_dp * (n_seq - 1) - (1 if n_seq > 1 else 0), 0)

    def cols(h):
        return pl.ds(h * DH if isinstance(h, int) else pl.multiple_of(h * DH, DH), DH)

    def piece(part):
        return pl.ds(part * rows, rows)

    def forward(h, part):
        return pltpu.make_async_remote_copy(
            src_ref=fsend.at[h, piece(part)], dst_ref=frecv.at[h, piece(part)],
            send_sem=fs_sem.at[h, part], recv_sem=fr_sem.at[h, part],
            device_id={"seq": place + 1}, device_id_type=MESH,
        )

    def backward(h, part):
        return pltpu.make_async_remote_copy(
            src_ref=bsend.at[h, piece(part)], dst_ref=brecv.at[h, piece(part)],
            send_sem=bs_sem.at[h, part], recv_sem=br_sem.at[h, part],
            device_id={"seq": place - 1}, device_id_type=MESH,
        )

    def each_head(body):
        def step(h, carry):
            body(h)
            return carry

        lax.fori_loop(0, heads, step, 0)

    loads[0].wait()
    starts_at = []
    starts = jnp.int32(0)
    for j in range(off_ref.shape[1]):
        offset = off_ref[0, j]
        starts_at.append(jnp.where(offset < BLK, j * BLK + offset, length))
        starts = starts + jnp.where(offset < BLK, 1, 0)

    def labels(positions):
        total = jnp.zeros(positions.shape, jnp.int32)
        for at in starts_at:
            total = total + jnp.where(positions >= at, 1, 0)
        return total

    label = labels(lax.broadcasted_iota(jnp.int32, (length, DH), 0))
    head_ref[...] = jnp.where(label == 0, 1.0, 0.0).astype(BF16)
    tail_ref[...] = jnp.where(label == starts, 1.0, 0.0).astype(BF16)

    def passed(own, come):
        keep = jnp.full(come.shape, starts, jnp.int32) == 0
        return own + jnp.where(keep, come, 0.0)

    loads[1].wait()
    loads[2].wait()

    def tail(h):
        fsend[h] = dot(k_ref[:, cols(h)] * tail_ref[...], v_ref[:, cols(h)], 0, 0)

    def launch(h):
        @pl.when(first & (n_seq > 1))
        def _():
            for part in range(CUTS):
                forward(h, part).start()

    tail(0)
    pl.semaphore_wait(barrier, greeted)
    launch(0)

    def tails(h, carry):
        tail(h)
        launch(h)
        return carry

    lax.fori_loop(1, heads, tails, 0)

    rows_at = lax.broadcasted_iota(jnp.int32, (length, length), 0)
    cols_at = lax.broadcasted_iota(jnp.int32, (length, length), 1)
    allow_ref[...] = jnp.where(
        (labels(rows_at) == labels(cols_at)) & (cols_at <= rows_at), 1.0, 0.0
    )

    @pl.when(first)
    def _():
        frecv[...] = jnp.zeros_like(frecv)

    @pl.when(last)
    def _():
        brecv[...] = jnp.zeros_like(brecv)

    sq_ref[...] = jnp.zeros_like(sq_ref)
    raw_ref[...] = jnp.zeros_like(raw_ref)
    for load in loads[3:]:
        load.wait()

    def relay_right(h, part):
        @pl.when(jnp.logical_not(first))
        def _():
            forward(h, part).wait_recv()

            @pl.when(jnp.logical_not(last))
            def _():
                fsend[h, piece(part)] = passed(fsend[h, piece(part)], frecv[h, piece(part)])
                forward(h, part).start()

    def attend(h):
        scores = dot(q_ref[:, cols(h)], k_ref[:, cols(h)], 1, 1)
        wts_ref[h] = (scores * allow_ref[...]).astype(BF16)
        att_ref[:, cols(h)] = dot(wts_ref[h], v_ref[:, cols(h)], 1, 0)

    def add_carried(h):
        attended = att_ref[:, cols(h)] + dot(
            q_ref[:, cols(h)] * head_ref[...], frecv[h].astype(BF16), 1, 0
        )
        att_ref[:, cols(h)] = attended
        sq_ref[...] = sq_ref[...] + attended * attended
        raw_ref[...] = raw_ref[...] + gain_ref[:, cols(h)] * g_ref[:, cols(h)].astype(F32) * attended

    def staggered(ahead, local, relay, finish, passed_on):
        def before(h, carry):
            local(h)
            return carry

        lax.fori_loop(0, ahead, before, 0)

        @pl.when(first | last)
        def _():
            def step(h):
                for part in range(CUTS):
                    relay(h, part)
                finish(h)

            each_head(step)

        @pl.when(jnp.logical_not(first | last))
        def _():
            def step(h):
                for part in range(CUTS):
                    relay(h, part)

            each_head(step)
            passed_on()

            def rest(h):
                @pl.when(h >= ahead)
                def _():
                    local(h)

                finish(h)

            each_head(rest)

    ahead = jnp.where(first | last, heads, jnp.minimum(2 * place - 1, heads))
    staggered(ahead, attend, relay_right, add_carried, lambda: None)

    stats[ten, 0:1, :] = jnp.sum(sq_ref[...].T, axis=0, keepdims=True)
    stats[ten, 1:2, :] = jnp.sum(raw_ref[...].T, axis=0, keepdims=True)

    def exchange(turn, slot):
        return pltpu.make_async_remote_copy(
            src_ref=stats.at[slot], dst_ref=stats.at[slot],
            send_sem=ss_sem.at[turn], recv_sem=sr_sem.at[slot],
            device_id={"tensor": lax.rem(ten + turn, n_ten)}, device_id_type=MESH,
        )

    for turn in range(1, n_ten):
        exchange(turn, ten).start()
    for turn in range(1, n_ten):
        exchange(turn, lax.rem(ten + turn, n_ten)).wait_recv()
    totals = stats[0]
    for t in range(1, n_ten):
        totals = totals + stats[t]
    inverse = lax.rsqrt(totals[0:1, :] / CH + EPS)
    slope = inverse * inverse * (totals[1:2, :] / CH)
    sq_ref[...] = jnp.broadcast_to(inverse, (DH, length)).T
    raw_ref[...] = jnp.broadcast_to(slope, (DH, length)).T

    def before_norm(h):
        upstream = g_ref[:, cols(h)].astype(F32)
        pre = sq_ref[...] * (gain_ref[:, cols(h)] * upstream - att_ref[:, cols(h)] * raw_ref[...])
        pre = pre.astype(BF16)
        pre_ref[:, cols(h)] = pre
        bsend[h] = dot(q_ref[:, cols(h)] * head_ref[...], pre, 0, 0)

        @pl.when(last & (n_seq > 1))
        def _():
            for part in range(CUTS):
                backward(h, part).start()

    each_head(before_norm)

    def after_norm(h):
        normed = att_ref[:, cols(h)] * sq_ref[...]
        out_ref[:, cols(h)] = (gain_ref[:, cols(h)] * normed).astype(BF16)
        gain_own[:, cols(h)] = jnp.sum(
            g_ref[:, cols(h)].astype(F32) * normed, axis=0, keepdims=True
        )

    for h in range(heads):
        after_norm(h)

    gain_right = pltpu.make_async_remote_copy(
        src_ref=gain_own, dst_ref=gain_come, send_sem=right_sem.at[0], recv_sem=right_sem.at[1],
        device_id={"seq": place + 1}, device_id_type=MESH,
    )
    def gain_out(turn):
        other = lax.rem(mine * n_seq + place + turn, group)
        return pltpu.make_async_remote_copy(
            src_ref=gain_dp.at[mine], dst_ref=gain_dp.at[mine],
            send_sem=left_sem.at[turn], recv_sem=dp_sem.at[mine],
            device_id={"dp": lax.div(other, n_seq), "seq": lax.rem(other, n_seq)}, device_id_type=MESH,
        )

    def gain_in(d):
        return pltpu.make_async_remote_copy(
            src_ref=gain_dp.at[d], dst_ref=gain_dp.at[d],
            send_sem=left_sem.at[0], recv_sem=dp_sem.at[d],
            device_id={"seq": 0}, device_id_type=MESH,
        )

    @pl.when(jnp.logical_not(first))
    def _():
        gain_right.wait_recv()
        gain_own[...] = gain_own[...] + gain_come[...]

    @pl.when(jnp.logical_not(last))
    def _():
        gain_right.start()

    @pl.when(last)
    def _():
        gain_dp[mine] = gain_own[...]

        def send(turn, carry):
            gain_out(turn).start()
            return carry

        lax.fori_loop(1, group, send, 0)

    def relay_left(h, part):
        @pl.when(jnp.logical_not(last))
        def _():
            backward(h, part).wait_recv()

            @pl.when(jnp.logical_not(first))
            def _():
                bsend[h, piece(part)] = passed(bsend[h, piece(part)], brecv[h, piece(part)])
                backward(h, part).start()

    def local_grads(h):
        pre = pre_ref[:, cols(h)]
        grad_weights = (dot(pre, v_ref[:, cols(h)], 1, 1) * allow_ref[...]).astype(BF16)
        gq = dot(grad_weights, k_ref[:, cols(h)], 1, 0)
        gq = gq + dot(pre * head_ref[...], frecv[h].astype(BF16), 1, 1)
        gq_ref[:, cols(h)] = gq.astype(BF16)
        pk_ref[:, cols(h)] = dot(grad_weights, q_ref[:, cols(h)], 0, 0)

        pv_ref[:, cols(h)] = dot(wts_ref[h], pre, 0, 0)

    def finish(h):
        later = brecv[h].astype(BF16)
        gk = pk_ref[:, cols(h)] + dot(v_ref[:, cols(h)] * tail_ref[...], later, 1, 1)
        gk_ref[:, cols(h)] = gk.astype(BF16)
        gv = pv_ref[:, cols(h)] + dot(k_ref[:, cols(h)] * tail_ref[...], later, 1, 0)
        gv_ref[:, cols(h)] = gv.astype(BF16)

    ahead = jnp.where(first | last, heads, jnp.minimum(n_seq - 1 - place, heads))
    staggered(ahead, local_grads, relay_left, finish, lambda: None)

    for d in range(n_dp):
        @pl.when(jnp.logical_not(last & (mine == d)))
        def _():
            gain_in(d).wait_recv()

    total = gain_dp[0]
    for d in range(1, n_dp):
        total = total + gain_dp[d]
    gg_ref[...] = total

    @pl.when(last)
    def _():
        def sent(turn, carry):
            gain_out(turn).wait_send()
            return carry

        lax.fori_loop(1, group, sent, 0)

    for turn in range(1, n_ten):
        exchange(turn, ten).wait_send()

    @pl.when(jnp.logical_not(last))
    def _():
        for h in range(heads):
            for part in range(CUTS):
                forward(h, part).wait_send()
        gain_right.wait_send()

    @pl.when(jnp.logical_not(first))
    def _():
        for h in range(heads):
            for part in range(CUTS):
                backward(h, part).wait_send()


def hand_out(*refs):
    count = len(refs) // 2
    copies = [
        pltpu.make_async_copy(refs[i], refs[count + i], refs[-1].at[i]) for i in range(count)
    ]
    for copy in copies:
        copy.start()
    for copy in copies:
        copy.wait()


def solution(mesh):
    sizes = (mesh.shape["dp"], mesh.shape["seq"], mesh.shape["tensor"])

    def shards(query, key_rows, value, gain, grad_out, start_offset):
        _, length, width = query.shape
        heads = width // DH
        hbm = pl.BlockSpec(memory_space=pltpu.HBM)
        vmem = pl.BlockSpec(memory_space=pltpu.VMEM)
        rows = jax.ShapeDtypeStruct((length, width), BF16)
        shapes = (rows,) * 4 + (jax.ShapeDtypeStruct((1, width), F32),)
        dma = pltpu.SemaphoreType.DMA
        flat = lambda a: a.reshape(length, width)
        outs = pl.pallas_call(
            functools.partial(kernel, sizes),
            out_shape=tuple(pltpu.VMEM(a.shape, a.dtype) for a in shapes),
            in_specs=[hbm] * 6,
            out_specs=(vmem,) * 5,
            scratch_shapes=[pltpu.SMEM(start_offset.shape, jnp.int32), pltpu.VMEM((1, width), F32)]
            + [pltpu.VMEM((length, width), BF16)] * 4
            + [
                pltpu.VMEM((length, length), F32),
                pltpu.VMEM((length, DH), BF16),
                pltpu.VMEM((length, DH), BF16),
                pltpu.VMEM((heads, length, length), BF16),
                pltpu.VMEM((length, width), F32),
                pltpu.VMEM((length, width), BF16),
                pltpu.VMEM((length, width), F32),
                pltpu.VMEM((length, width), F32),
                pltpu.VMEM((length, DH), F32),
                pltpu.VMEM((length, DH), F32),
            ]
            + [pltpu.VMEM((heads, DH, DH), F32)] * 4
            + [pltpu.VMEM((sizes[2], 2, length), F32), pltpu.VMEM((1, width), F32), pltpu.VMEM((1, width), F32)]
            + [pltpu.VMEM((sizes[0], 1, width), F32)]
            + [dma((6,))] + [dma((heads, CUTS))] * 4
            + [dma((sizes[2],)), dma((sizes[2],)), dma((sizes[0] * sizes[1],)), dma((sizes[0],)), dma((2,))],
            compiler_params=pltpu.CompilerParams(
                collective_id=0, has_side_effects=True, vmem_limit_bytes=61 * 1024 * 1024
            ),
        )(start_offset, gain.reshape(1, width), flat(query), flat(key_rows), flat(value), flat(grad_out))
        *outs, grad_gain = pl.pallas_call(
            hand_out,
            out_shape=shapes,
            in_specs=[vmem] * 5,
            out_specs=(hbm,) * 5,
            scratch_shapes=[dma((5,))],
            compiler_params=pltpu.CompilerParams(vmem_limit_bytes=8 * 1024 * 1024),
        )(*outs)
        return tuple(a.reshape(1, length, width) for a in outs) + (grad_gain.reshape(width),)

    split = P("dp", "seq", "tensor")
    return jax.shard_map(
        shards,
        mesh=mesh,
        in_specs=(split, split, split, P("tensor"), split, P("dp", "seq")),
        out_specs=(split, split, split, split, P("tensor")),
        check_vma=False,
    )
```

```python
import functools

import jax
import jax.numpy as jnp
from jax import lax
from jax.experimental import pallas as pl
from jax.experimental.pallas import tpu as pltpu
from jax.sharding import PartitionSpec as P

DH = 128
BLK = 64
CH = 2048
EPS = 1e-05
CUTS = 4

MESH = pl.DeviceIdType.MESH
F32 = jnp.float32
BF16 = jnp.bfloat16


def dot(a, b, over_a, over_b):
    return lax.dot_general(a, b, (((over_a,), (over_b,)), ((), ())), preferred_element_type=F32)


def kernel(
    sizes, off_hbm, gain_hbm, q_hbm, k_hbm, v_hbm, g_hbm,
    out_ref, gq_ref, gk_ref, gv_ref, gg_ref,
    off_ref, gain_ref, q_ref, k_ref, v_ref, g_ref,
    allow_ref, head_ref, tail_ref, wts_ref, att_ref, pre_ref, pk_ref, pv_ref, sq_ref, raw_ref,
    fsend, frecv, bsend, brecv, stats, gain_own, gain_come, gain_dp,
    in_sem, fs_sem, fr_sem, bs_sem, br_sem, ss_sem, sr_sem, left_sem, dp_sem, right_sem, turn_sem,
):
    n_dp, n_seq, n_ten = sizes
    length, width = q_ref.shape
    heads = width // DH
    rows = DH // CUTS
    place = lax.axis_index("seq")
    ten = lax.axis_index("tensor")
    mine = lax.axis_index("dp")
    first, last = place == 0, place == n_seq - 1
    back = n_seq - 1 - place
    group = n_dp * n_seq

    loads = [
        pltpu.make_async_copy(src, dst, in_sem.at[i])
        for i, (src, dst) in enumerate(
            (
                (off_hbm, off_ref), (k_hbm, k_ref), (v_hbm, v_ref),
                (q_hbm, q_ref), (g_hbm, g_ref), (gain_hbm, gain_ref),
            )
        )
    ]
    for load in loads:
        load.start()

    barrier = pltpu.get_barrier_semaphore()

    def greet(device):
        pl.semaphore_signal(barrier, inc=1, device_id=device, device_id_type=MESH)

    @pl.when(jnp.logical_not(last))
    def _():
        greet({"seq": place + 1})

    @pl.when(jnp.logical_not(first))
    def _():
        greet({"seq": place - 1})

    for turn in range(1, n_ten):
        greet({"tensor": lax.rem(ten + turn, n_ten)})
    for turn in range(1, n_dp):
        greet({"dp": lax.rem(mine + turn, n_dp)})

    for d in range(n_dp):
        @pl.when((back > 1) | ((back == 1) & (mine != d)))
        def _():
            greet({"dp": d, "seq": n_seq - 1})

    greeted = n_ten - 1 + n_dp - 1 + jnp.where(last, 0, 1) + jnp.where(first, 0, 1)
    greeted = greeted + jnp.where(last, n_dp * (n_seq - 1) - (1 if n_seq > 1 else 0), 0)

    def cols(h):
        return pl.ds(h * DH if isinstance(h, int) else pl.multiple_of(h * DH, DH), DH)

    def piece(part):
        return pl.ds(part * rows, rows)

    def forward(h, part):
        return pltpu.make_async_remote_copy(
            src_ref=fsend.at[h, piece(part)], dst_ref=frecv.at[h, piece(part)],
            send_sem=fs_sem.at[h, part], recv_sem=fr_sem.at[h, part],
            device_id={"seq": place + 1}, device_id_type=MESH,
        )

    def backward(h, part):
        return pltpu.make_async_remote_copy(
            src_ref=bsend.at[h, piece(part)], dst_ref=brecv.at[h, piece(part)],
            send_sem=bs_sem.at[h, part], recv_sem=br_sem.at[h, part],
            device_id={"seq": place - 1}, device_id_type=MESH,
        )

    def each_head(body):
        def step(h, carry):
            body(h)
            return carry

        lax.fori_loop(0, heads, step, 0)

    loads[0].wait()
    starts_at = []
    starts = jnp.int32(0)
    for j in range(off_ref.shape[1]):
        offset = off_ref[0, j]
        starts_at.append(jnp.where(offset < BLK, j * BLK + offset, length))
        starts = starts + jnp.where(offset < BLK, 1, 0)

    def labels(positions):
        total = jnp.zeros(positions.shape, jnp.int32)
        for at in starts_at:
            total = total + jnp.where(positions >= at, 1, 0)
        return total

    label = labels(lax.broadcasted_iota(jnp.int32, (length, DH), 0))
    head_ref[...] = jnp.where(label == 0, 1.0, 0.0).astype(BF16)
    tail_ref[...] = jnp.where(label == starts, 1.0, 0.0).astype(BF16)

    def passed(own, come):
        keep = jnp.full(come.shape, starts, jnp.int32) == 0
        return own + jnp.where(keep, come, 0.0)

    loads[1].wait()
    loads[2].wait()

    def tail(h):
        fsend[h] = dot(k_ref[:, cols(h)] * tail_ref[...], v_ref[:, cols(h)], 0, 0)

    leads = first & (mine < n_dp - 1) & (n_seq > 1)
    follows = first & (mine > 0) & (n_seq > 1)

    def launch(h):
        @pl.when(first & (mine == 0) & (n_seq > 1))
        def _():
            for part in range(CUTS):
                forward(h, part).start()

    tail(0)
    pl.semaphore_wait(barrier, greeted)
    launch(0)

    def tails(h, carry):
        tail(h)
        launch(h)
        return carry

    lax.fori_loop(1, heads, tails, 0)

    @pl.when(follows)
    def _():
        pl.semaphore_wait(turn_sem, 1)
        for h in range(heads):
            for part in range(CUTS):
                forward(h, part).start()

    @pl.when(leads)
    def _():
        for h in range(heads // 2):
            for part in range(CUTS):
                forward(h, part).wait_send()
        pl.semaphore_signal(turn_sem, inc=1, device_id={"dp": mine + 1}, device_id_type=MESH)

    rows_at = lax.broadcasted_iota(jnp.int32, (length, length), 0)
    cols_at = lax.broadcasted_iota(jnp.int32, (length, length), 1)
    allow_ref[...] = jnp.where(
        (labels(rows_at) == labels(cols_at)) & (cols_at <= rows_at), 1.0, 0.0
    )

    @pl.when(first)
    def _():
        frecv[...] = jnp.zeros_like(frecv)

    @pl.when(last)
    def _():
        brecv[...] = jnp.zeros_like(brecv)

    sq_ref[...] = jnp.zeros_like(sq_ref)
    raw_ref[...] = jnp.zeros_like(raw_ref)
    for load in loads[3:]:
        load.wait()

    def relay_right(h, part):
        @pl.when(jnp.logical_not(first))
        def _():
            forward(h, part).wait_recv()

            @pl.when(jnp.logical_not(last))
            def _():
                fsend[h, piece(part)] = passed(fsend[h, piece(part)], frecv[h, piece(part)])
                forward(h, part).start()

    def attend(h):
        scores = dot(q_ref[:, cols(h)], k_ref[:, cols(h)], 1, 1)
        wts_ref[h] = (scores * allow_ref[...]).astype(BF16)
        att_ref[:, cols(h)] = dot(wts_ref[h], v_ref[:, cols(h)], 1, 0)

    def add_carried(h):
        attended = att_ref[:, cols(h)] + dot(
            q_ref[:, cols(h)] * head_ref[...], frecv[h].astype(BF16), 1, 0
        )
        att_ref[:, cols(h)] = attended
        sq_ref[...] = sq_ref[...] + attended * attended
        raw_ref[...] = raw_ref[...] + gain_ref[:, cols(h)] * g_ref[:, cols(h)].astype(F32) * attended

    def staggered(ahead, local, relay, finish, passed_on):
        def before(h, carry):
            local(h)
            return carry

        lax.fori_loop(0, ahead, before, 0)

        @pl.when(first | last)
        def _():
            def step(h):
                for part in range(CUTS):
                    relay(h, part)
                finish(h)

            each_head(step)

        @pl.when(jnp.logical_not(first | last))
        def _():
            def step(h):
                for part in range(CUTS):
                    relay(h, part)

            each_head(step)
            passed_on()

            def rest(h):
                @pl.when(h >= ahead)
                def _():
                    local(h)

                finish(h)

            each_head(rest)

    ahead = jnp.where(first | last, heads, jnp.minimum(2 * place - 1, heads))
    staggered(ahead, attend, relay_right, add_carried, lambda: None)

    stats[ten, 0:1, :] = jnp.sum(sq_ref[...].T, axis=0, keepdims=True)
    stats[ten, 1:2, :] = jnp.sum(raw_ref[...].T, axis=0, keepdims=True)

    def exchange(turn, slot):
        return pltpu.make_async_remote_copy(
            src_ref=stats.at[slot], dst_ref=stats.at[slot],
            send_sem=ss_sem.at[turn], recv_sem=sr_sem.at[slot],
            device_id={"tensor": lax.rem(ten + turn, n_ten)}, device_id_type=MESH,
        )

    for turn in range(1, n_ten):
        exchange(turn, ten).start()
    for turn in range(1, n_ten):
        exchange(turn, lax.rem(ten + turn, n_ten)).wait_recv()
    totals = stats[0]
    for t in range(1, n_ten):
        totals = totals + stats[t]
    inverse = lax.rsqrt(totals[0:1, :] / CH + EPS)
    slope = inverse * inverse * (totals[1:2, :] / CH)
    sq_ref[...] = jnp.broadcast_to(inverse, (DH, length)).T
    raw_ref[...] = jnp.broadcast_to(slope, (DH, length)).T

    def before_norm(h):
        upstream = g_ref[:, cols(h)].astype(F32)
        pre = sq_ref[...] * (gain_ref[:, cols(h)] * upstream - att_ref[:, cols(h)] * raw_ref[...])
        pre = pre.astype(BF16)
        pre_ref[:, cols(h)] = pre
        bsend[h] = dot(q_ref[:, cols(h)] * head_ref[...], pre, 0, 0)

        @pl.when(last & (n_seq > 1))
        def _():
            for part in range(CUTS):
                backward(h, part).start()

    each_head(before_norm)

    def after_norm(h):
        normed = att_ref[:, cols(h)] * sq_ref[...]
        out_ref[:, cols(h)] = (gain_ref[:, cols(h)] * normed).astype(BF16)
        gain_own[:, cols(h)] = jnp.sum(
            g_ref[:, cols(h)].astype(F32) * normed, axis=0, keepdims=True
        )

    for h in range(heads):
        after_norm(h)

    gain_right = pltpu.make_async_remote_copy(
        src_ref=gain_own, dst_ref=gain_come, send_sem=right_sem.at[0], recv_sem=right_sem.at[1],
        device_id={"seq": place + 1}, device_id_type=MESH,
    )
    def gain_out(turn):
        other = lax.rem(mine * n_seq + place + turn, group)
        return pltpu.make_async_remote_copy(
            src_ref=gain_dp.at[mine], dst_ref=gain_dp.at[mine],
            send_sem=left_sem.at[turn], recv_sem=dp_sem.at[mine],
            device_id={"dp": lax.div(other, n_seq), "seq": lax.rem(other, n_seq)}, device_id_type=MESH,
        )

    def gain_in(d):
        return pltpu.make_async_remote_copy(
            src_ref=gain_dp.at[d], dst_ref=gain_dp.at[d],
            send_sem=left_sem.at[0], recv_sem=dp_sem.at[d],
            device_id={"seq": 0}, device_id_type=MESH,
        )

    @pl.when(jnp.logical_not(first))
    def _():
        gain_right.wait_recv()
        gain_own[...] = gain_own[...] + gain_come[...]

    @pl.when(jnp.logical_not(last))
    def _():
        gain_right.start()

    @pl.when(last)
    def _():
        gain_dp[mine] = gain_own[...]

        def send(turn, carry):
            gain_out(turn).start()
            return carry

        lax.fori_loop(1, group, send, 0)

    def relay_left(h, part):
        @pl.when(jnp.logical_not(last))
        def _():
            backward(h, part).wait_recv()

            @pl.when(jnp.logical_not(first))
            def _():
                bsend[h, piece(part)] = passed(bsend[h, piece(part)], brecv[h, piece(part)])
                backward(h, part).start()

    def local_grads(h):
        pre = pre_ref[:, cols(h)]
        grad_weights = (dot(pre, v_ref[:, cols(h)], 1, 1) * allow_ref[...]).astype(BF16)
        gq = dot(grad_weights, k_ref[:, cols(h)], 1, 0)
        gq = gq + dot(pre * head_ref[...], frecv[h].astype(BF16), 1, 1)
        gq_ref[:, cols(h)] = gq.astype(BF16)
        pk_ref[:, cols(h)] = dot(grad_weights, q_ref[:, cols(h)], 0, 0)

        pv_ref[:, cols(h)] = dot(wts_ref[h], pre, 0, 0)

    def finish(h):
        later = brecv[h].astype(BF16)
        gk = pk_ref[:, cols(h)] + dot(v_ref[:, cols(h)] * tail_ref[...], later, 1, 1)
        gk_ref[:, cols(h)] = gk.astype(BF16)
        gv = pv_ref[:, cols(h)] + dot(k_ref[:, cols(h)] * tail_ref[...], later, 1, 0)
        gv_ref[:, cols(h)] = gv.astype(BF16)

    ahead = jnp.where(first | last, heads, jnp.minimum(n_seq - 1 - place, heads))
    staggered(ahead, local_grads, relay_left, finish, lambda: None)

    for d in range(n_dp):
        @pl.when(jnp.logical_not(last & (mine == d)))
        def _():
            gain_in(d).wait_recv()

    total = gain_dp[0]
    for d in range(1, n_dp):
        total = total + gain_dp[d]
    gg_ref[...] = total

    @pl.when(last)
    def _():
        def sent(turn, carry):
            gain_out(turn).wait_send()
            return carry

        lax.fori_loop(1, group, sent, 0)

    for turn in range(1, n_ten):
        exchange(turn, ten).wait_send()

    @pl.when(jnp.logical_not(last))
    def _():
        @pl.when(jnp.logical_not(leads))
        def _():
            for h in range(heads // 2):
                for part in range(CUTS):
                    forward(h, part).wait_send()

        for h in range(heads // 2, heads):
            for part in range(CUTS):
                forward(h, part).wait_send()
        gain_right.wait_send()

    @pl.when(jnp.logical_not(first))
    def _():
        for h in range(heads):
            for part in range(CUTS):
                backward(h, part).wait_send()


def hand_out(*refs):
    count = len(refs) // 2
    copies = [
        pltpu.make_async_copy(refs[i], refs[count + i], refs[-1].at[i]) for i in range(count)
    ]
    for copy in copies:
        copy.start()
    for copy in copies:
        copy.wait()


def solution(mesh):
    sizes = (mesh.shape["dp"], mesh.shape["seq"], mesh.shape["tensor"])

    def shards(query, key_rows, value, gain, grad_out, start_offset):
        _, length, width = query.shape
        heads = width // DH
        hbm = pl.BlockSpec(memory_space=pltpu.HBM)
        vmem = pl.BlockSpec(memory_space=pltpu.VMEM)
        rows = jax.ShapeDtypeStruct((length, width), BF16)
        shapes = (rows,) * 4 + (jax.ShapeDtypeStruct((1, width), F32),)
        dma = pltpu.SemaphoreType.DMA
        flat = lambda a: a.reshape(length, width)
        outs = pl.pallas_call(
            functools.partial(kernel, sizes),
            out_shape=tuple(pltpu.VMEM(a.shape, a.dtype) for a in shapes),
            in_specs=[hbm] * 6,
            out_specs=(vmem,) * 5,
            scratch_shapes=[pltpu.SMEM(start_offset.shape, jnp.int32), pltpu.VMEM((1, width), F32)]
            + [pltpu.VMEM((length, width), BF16)] * 4
            + [
                pltpu.VMEM((length, length), F32),
                pltpu.VMEM((length, DH), BF16),
                pltpu.VMEM((length, DH), BF16),
                pltpu.VMEM((heads, length, length), BF16),
                pltpu.VMEM((length, width), F32),
                pltpu.VMEM((length, width), BF16),
                pltpu.VMEM((length, width), F32),
                pltpu.VMEM((length, width), F32),
                pltpu.VMEM((length, DH), F32),
                pltpu.VMEM((length, DH), F32),
            ]
            + [pltpu.VMEM((heads, DH, DH), F32)] * 4
            + [pltpu.VMEM((sizes[2], 2, length), F32), pltpu.VMEM((1, width), F32), pltpu.VMEM((1, width), F32)]
            + [pltpu.VMEM((sizes[0], 1, width), F32)]
            + [dma((6,))] + [dma((heads, CUTS))] * 4
            + [dma((sizes[2],)), dma((sizes[2],)), dma((sizes[0] * sizes[1],)), dma((sizes[0],)), dma((2,))]
            + [pltpu.SemaphoreType.REGULAR],
            compiler_params=pltpu.CompilerParams(
                collective_id=0, has_side_effects=True, vmem_limit_bytes=61 * 1024 * 1024
            ),
        )(start_offset, gain.reshape(1, width), flat(query), flat(key_rows), flat(value), flat(grad_out))
        *outs, grad_gain = pl.pallas_call(
            hand_out,
            out_shape=shapes,
            in_specs=[vmem] * 5,
            out_specs=(hbm,) * 5,
            scratch_shapes=[dma((5,))],
            compiler_params=pltpu.CompilerParams(vmem_limit_bytes=8 * 1024 * 1024),
        )(*outs)
        return tuple(a.reshape(1, length, width) for a in outs) + (grad_gain.reshape(width),)

    split = P("dp", "seq", "tensor")
    return jax.shard_map(
        shards,
        mesh=mesh,
        in_specs=(split, split, split, P("tensor"), split, P("dp", "seq")),
        out_specs=(split, split, split, split, P("tensor")),
        check_vma=False,
    )
```
